32 devices in a mesh: replica: 4 (over y, x), shard: 8 (over z, core).
Axes of the slice: x: 2, y: 2, z: 4, core: 2. Of those that a mesh axis runs over, the one named last changes fastest.
Arguments:
- hidden_in: float32 [96, 256, 768], P(('replica', 'shard')), may hold values from -1.7 to 1.7
- condition: float32 [96, 768], P(('replica', 'shard')), may hold values from -1.7 to 1.7
- latent_live: int32 [96], P(('replica', 'shard')), may hold values from 0 to 1, as said below
- out_grad: float32 [96, 256, 768], P(('replica', 'shard')), may hold values from -1.7 to 1.7
- ada_weight: float32 [2, 768, 4608], P(None, 'shard'), may hold values from -0.21875 to 0.21875
- qkv_weight: float32 [2, 768, 2304], P(None, 'shard'), may hold values from -0.21875 to 0.21875
- proj_weight: float32 [2, 768, 768], P(None, 'shard'), may hold values from -0.875 to 0.875
- fc1_weight: float32 [2, 768, 3072], P(None, 'shard'), may hold values from -0.21875 to 0.21875
- fc2_weight: float32 [2, 3072, 768], P(None, 'shard'), may hold values from -0.109375 to 0.109375
- ada_bias: float32 [2, 4608], P(None, 'shard'), may hold values from -0.8 to 0.8
- qv_bias: float32 [2, 1536], P(None, 'shard'), may hold values from -0.8 to 0.8
- proj_bias: float32 [2, 768], P(None, 'shard'), may hold values from -0.8 to 0.8
- fc1_bias: float32 [2, 3072], P(None, 'shard'), may hold values from -0.8 to 0.8
- fc2_bias: float32 [2, 768], P(None, 'shard'), may hold values from -0.8 to 0.8
Outputs:
- out_hidden: float32 [96, 256, 768], P(('replica', 'shard'))
- grad_hidden: float32 [96, 256, 768], P(('replica', 'shard'))
- grad_condition: float32 [96, 768], P(('replica', 'shard'))
- grad_ada_weight: float32 [2, 768, 4608], P(None, 'shard')
- grad_qkv_weight: float32 [2, 768, 2304], P(None, 'shard')
- grad_proj_weight: float32 [2, 768, 768], P(None, 'shard')
- grad_fc1_weight: float32 [2, 768, 3072], P(None, 'shard')
- grad_fc2_weight: float32 [2, 3072, 768], P(None, 'shard')
- grad_ada_bias: float32 [2, 4608], P(None, 'shard')
- grad_qv_bias: float32 [2, 1536], P(None, 'shard')
- grad_proj_bias: float32 [2, 768], P(None, 'shard')
- grad_fc1_bias: float32 [2, 3072], P(None, 'shard')
- grad_fc2_bias: float32 [2, 768], P(None, 'shard')
The draws below stay inside these ranges and needn't reach their ends.
Inputs may be any that keep to these rules, and one draw needn't show every extreme that they name: `latent_live`: slot i holds a latent whenever i is a multiple of 3; the other slots may be empty.
All inputs are finite; a program needn't handle non-finite values.
Results may differ from the reference program's by a relative error of at most 0.013.
The reference program's roundings to bfloat16 on the way count: a program that leaves them out, or rounds other values in their place, can miss the bound.
Values may be sent and summed in bfloat16 or wider, within the bound.
No kernel may reach another device: no remote copies, remote signals or barrier semaphores. Data moves between devices by JAX's collectives and lax.ppermute only.
A program may use at most 256 MiB of HBM per device.

```python
import math
import jax
import jax.numpy as jnp
from jax import lax

D = 768
HEADS = 12
HEAD_DIM = 64
FF = 3072
SEQ = 256
LAT_DEV = 3
LAYERS = 2
LATENTS = 96


def draw_latent_live(key, part):
    extra = jax.random.randint(key, (LATENTS,), 0, 2)
    leading = jnp.arange(LATENTS) % LAT_DEV == 0
    return jnp.where(leading, 1, extra).astype(jnp.int32)


def shard_levels(key, extent, cuts, smallest, largest):
    factor_of = 1.0
    for dim, shards_of in cuts:
        draws = jax.random.uniform(jax.random.fold_in(jax.random.fold_in(key, 6), dim), (shards_of,), jnp.float32, smallest / len(cuts), largest / len(cuts))
        factor_of = factor_of * jnp.repeat(jnp.exp(draws), extent[dim] // shards_of).reshape((-1,) + (1,) * (len(extent) - 1 - dim))
    return factor_of


def normal_values(rng, dims, scale, reach, cuts=(), dtype=jnp.bfloat16):
    values = jax.random.normal(rng, dims, jnp.float32) * scale
    if len(cuts) > 0:
        values = shard_levels(rng, dims, cuts, -0.22, 0.18) * values
    return jnp.clip(values, min=-reach, max=reach).astype(dtype)


def setup_inputs(seed: int = 0) -> dict:
    key_list = jax.random.split(jax.random.key(seed), 15)
    return {
        "hidden_in": jnp.clip(jax.random.uniform(key_list[0], (LATENTS, SEQ, D), jnp.float32, -1.7, 1.7) * shard_levels(key_list[0], (LATENTS, SEQ, D), ((0, 32),), -0.4, 0.0), -1.7, 1.7),
        "condition": jnp.clip(jax.random.uniform(key_list[1], (LATENTS, D), jnp.float32, -1.7, 1.7) * shard_levels(key_list[1], (LATENTS, D), ((0, 32),), -0.4, 0.0), -1.7, 1.7),
        "latent_live": draw_latent_live(jax.random.fold_in(key_list[14], 71), 0),
        "out_grad": jnp.clip(jax.random.uniform(key_list[3], (LATENTS, SEQ, D), jnp.float32, -1.7, 1.7) * shard_levels(key_list[3], (LATENTS, SEQ, D), ((0, 32),), -0.4, 0.0), -1.7, 1.7),
        "ada_weight": normal_values(key_list[4], (LAYERS, D, 6 * D), D ** -0.5, 0.21875, ((1, 8),), jnp.float32),
        "qkv_weight": normal_values(key_list[5], (LAYERS, D, 3 * D), D ** -0.5, 0.21875, ((1, 8),), jnp.float32),
        "proj_weight": normal_values(key_list[6], (LAYERS, D, D), (D // 16) ** -0.5, 0.875, ((1, 8),), jnp.float32),
        "fc1_weight": normal_values(key_list[7], (LAYERS, D, FF), D ** -0.5, 0.21875, ((1, 8),), jnp.float32),
        "fc2_weight": normal_values(key_list[8], (LAYERS, FF, D), FF ** -0.5, 0.109375, ((1, 8),), jnp.float32),
        "ada_bias": jnp.clip(jax.random.uniform(key_list[9], (LAYERS, 6 * D), jnp.float32, -0.8, 0.8) * shard_levels(key_list[9], (LAYERS, 6 * D), ((1, 8),), -0.4, 0.0), -0.8, 0.8),
        "qv_bias": jnp.clip(jax.random.uniform(key_list[10], (LAYERS, 2 * D), jnp.float32, -0.8, 0.8) * shard_levels(key_list[10], (LAYERS, 2 * D), ((1, 8),), -0.4, 0.0), -0.8, 0.8),
        "proj_bias": jnp.clip(jax.random.uniform(key_list[11], (LAYERS, D), jnp.float32, -0.8, 0.8) * shard_levels(key_list[11], (LAYERS, D), ((1, 8),), -0.4, 0.0), -0.8, 0.8),
        "fc1_bias": jnp.clip(jax.random.uniform(key_list[12], (LAYERS, FF), jnp.float32, -0.8, 0.8) * shard_levels(key_list[12], (LAYERS, FF), ((1, 8),), -0.4, 0.0), -0.8, 0.8),
        "fc2_bias": jnp.clip(jax.random.uniform(key_list[13], (LAYERS, D), jnp.float32, -0.8, 0.8) * shard_levels(key_list[13], (LAYERS, D), ((1, 8),), -0.4, 0.0), -0.8, 0.8),
    }


@jax.custom_vjp
def low(v):
    return lax.optimization_barrier(v.astype(jnp.bfloat16)).astype(jnp.float32)

@jax.custom_vjp
def low_back(v):
    return v

def low_keep(v):
    return (low(v), None)

def low_pass(kept, grad):
    return (grad,)

def back_keep(v):
    return (v, None)

def back_low(kept, grad):
    return (low(grad),)
low.defvjp(low_keep, low_pass)
low_back.defvjp(back_keep, back_low)
norm_eps = 1e-06
highest = lax.Precision.HIGHEST

def norm_mod(hidden, offset, stretch):
    average = lax.optimization_barrier(jnp.mean(hidden, axis=-1, keepdims=True))
    centred = hidden - average
    spread = lax.optimization_barrier(jnp.mean(centred * centred, axis=-1, keepdims=True))
    normed = centred * lax.rsqrt(spread + norm_eps)
    return normed * (1.0 + stretch[:, None, :]) + offset[:, None, :]

def project(left_side, right_side):
    return jnp.einsum('bsd,de->bse', left_side, right_side, precision=highest)

def forward_all(params, hidden, condition, live_rows):
    lowered = [low(weight_piece) for weight_piece in params]
    cond_low = low(jax.nn.silu(condition))
    latents_here, seq_len, model_width = hidden.shape
    current = hidden
    for layer_index in range(LAYERS):
        ada_w, qkv_w, proj_w, up_w, down_w, ada_b, qv_b, proj_b, up_b, down_b = [weight_piece[layer_index] for weight_piece in lowered]
        modulation = jnp.dot(cond_low, ada_w, precision=highest) + ada_b
        offset_one, stretch_one, gate_one, offset_two, stretch_two, gate_two = jnp.split(modulation, 6, axis=-1)
        normed_one = low(norm_mod(current, offset_one, stretch_one))
        bias_full = jnp.concatenate([qv_b[:model_width], jnp.zeros((model_width,), jnp.float32), qv_b[model_width:]])
        qkv_rows = low(low_back(project(normed_one, qkv_w) + bias_full))
        heads_view = qkv_rows.reshape(latents_here, seq_len, 3, HEADS, HEAD_DIM)
        queries = heads_view[:, :, 0]
        key_rows = heads_view[:, :, 1]
        value_rows = heads_view[:, :, 2]
        raw_scores = low_back(jnp.einsum('bqhd,bkhd->bhqk', queries, key_rows, precision=highest))
        attn_probs = jax.nn.softmax(raw_scores * HEAD_DIM ** (-0.5), axis=-1)
        mixed_heads = jnp.einsum('bhqk,bkhd->bqhd', low(attn_probs), value_rows, precision=highest)
        mixed_heads = low(low_back(mixed_heads.reshape(latents_here, seq_len, model_width)))
        branch_one = low_back(project(mixed_heads, proj_w) + proj_b)
        middle = current + gate_one[:, None, :] * branch_one
        normed_two = low(norm_mod(middle, offset_two, stretch_two))
        pre_act = low_back(project(normed_two, up_w) + up_b)
        act_rows = low(jax.nn.gelu(pre_act, approximate=True))
        branch_two = low_back(project(act_rows, down_w) + down_b)
        current = middle + gate_two[:, None, :] * branch_two
    return current * live_rows[:, None, None]

def reference(hidden_in, condition, latent_live, out_grad, ada_weight, qkv_weight, proj_weight, fc1_weight, fc2_weight, ada_bias, qv_bias, proj_bias, fc1_bias, fc2_bias):
    params = (ada_weight, qkv_weight, proj_weight, fc1_weight, fc2_weight, ada_bias, qv_bias, proj_bias, fc1_bias, fc2_bias)
    group_size = math.gcd(LATENTS, max(1, 4096 // SEQ))
    blocks = LATENTS // group_size

    def regroup(array):
        return array.reshape((blocks, group_size) + array.shape[1:])
    group_items = (regroup(hidden_in), regroup(condition), regroup(latent_live.astype(jnp.float32)), regroup(out_grad))

    def group_step(running, item):
        block_hidden, block_cond, block_live, block_grad = item

        def forward_block(weights, hidden, cond):
            return forward_all(weights, hidden, cond, block_live)
        outputs, pull_back = jax.vjp(forward_block, params, block_hidden, block_cond)
        grad_params, grad_in, grad_cond = pull_back(block_grad)
        running = tuple((before + extra for before, extra in zip(running, grad_params)))
        return (running, (outputs, grad_in, grad_cond))
    zero_grads = tuple((jnp.zeros_like(weight_piece) for weight_piece in params))
    running, (outputs, grad_in, grad_cond) = lax.scan(group_step, zero_grads, group_items)
    return (outputs.reshape(hidden_in.shape), grad_in.reshape(hidden_in.shape), grad_cond.reshape(condition.shape), running[0], running[1], running[2], running[3], running[4], running[5], running[6], running[7], running[8], running[9])
```

```python
import functools

import jax
import jax.numpy as jnp
from jax import lax
from jax.experimental import pallas as pl
from jax.experimental.pallas import tpu as pltpu
from jax.sharding import PartitionSpec as P

HEADS = 12
HEAD_DIM = 64
LAYERS = 2
SLABS = 4

norm_eps = 1e-06
highest = lax.Precision.HIGHEST
low_type = jnp.bfloat16
wide = jnp.float32


def nn(left, right):
    return lax.dot_general(left, right, (((1,), (0,)), ((), ())), preferred_element_type=wide)


def nt(left, right):
    return lax.dot_general(left, right, (((1,), (1,)), ((), ())), preferred_element_type=wide)


def tn(left, right):
    return lax.dot_general(left, right, (((0,), (0,)), ((), ())), preferred_element_type=wide)


def exact_lead(left_side, right_side):
    return lax.dot_general(
        left_side,
        right_side,
        (((0,), (0,)), ((), ())),
        precision=highest,
        preferred_element_type=wide,
    )


def exact_trail(left_side, right_side):
    return lax.dot_general(
        left_side,
        right_side,
        (((1,), (1,)), ((), ())),
        precision=highest,
        preferred_element_type=wide,
    )


def normalise(rows):
    centred = rows - jnp.mean(rows, axis=-1, keepdims=True)
    spread = jnp.mean(centred * centred, axis=-1, keepdims=True)
    inverse = lax.rsqrt(spread + norm_eps)
    return centred * inverse, inverse


def norm_back(grad, rows, stretch):
    normed, inverse = normalise(rows)
    inner = grad * (1.0 + stretch)
    first = jnp.mean(inner, axis=-1, keepdims=True)
    second = jnp.mean(inner * normed, axis=-1, keepdims=True)
    back = (inner - first - normed * second) * inverse
    return (
        back,
        jnp.sum(grad, axis=0, keepdims=True),
        jnp.sum(grad * normed, axis=0, keepdims=True),
    )


def qkv_kernel(x_ref, mod_ref, w_ref, b_ref, u_ref, qkv_ref):
    latents, seq, _ = x_ref.shape

    @pl.when(pl.program_id(0) == 0)
    def _():
        for i in range(latents):
            normed, _ = normalise(x_ref[i])
            u_ref[i * seq : (i + 1) * seq] = (
                normed * (1.0 + mod_ref[i, 1:2]) + mod_ref[i, 0:1]
            ).astype(low_type)

    for i in range(latents):
        part = slice(i * seq, (i + 1) * seq)
        qkv_ref[0, part] = (nn(u_ref[part], w_ref[0]) + b_ref[0]).astype(low_type)


def mix_kernel(qkv_ref, x_ref, mod_ref, w_ref, b_ref, o_ref, a_ref, x1_ref, u2_ref):
    seq, width = o_ref.shape
    pair = 2 * HEAD_DIM
    lane = lax.broadcasted_iota(jnp.int32, (seq, pair), 1)
    left = lane < HEAD_DIM
    for at in range(0, width, pair):
        query = qkv_ref[0, :, at : at + pair]
        key = qkv_ref[1, :, at : at + pair]
        value = qkv_ref[2, :, at : at + pair]
        mixed = []
        for side in (left, jnp.logical_not(left)):
            raw = nt(jnp.where(side, query, jnp.zeros_like(query)), key) * HEAD_DIM ** (-0.5)
            top = jnp.exp(raw - jnp.max(raw, axis=-1, keepdims=True))
            probs = top * (1.0 / jnp.sum(top, axis=-1, keepdims=True))
            mixed.append(nn(probs.astype(low_type), value))
        o_ref[:, at : at + pair] = jnp.where(left, mixed[0], mixed[1]).astype(low_type)
    branch = nn(o_ref[...], w_ref[0]) + b_ref[...]
    a_ref[...] = branch
    middle = x_ref[0] + mod_ref[0, 2:3] * branch
    x1_ref[...] = middle
    normed, _ = normalise(middle)
    u2_ref[...] = (normed * (1.0 + mod_ref[0, 4:5]) + mod_ref[0, 3:4]).astype(low_type)


GELU_SCALE = 0.7978845608028654
GELU_CUBE = 0.044715


def feed_kernel(
    u2_ref, x1_ref, mod_ref, up_ref, upb_ref, down_ref, downb_ref, g_ref, slope_ref, m_ref, x_ref
):
    latents = mod_ref.shape[0]
    seq = u2_ref.shape[0] // latents
    step = pl.program_id(0)
    for i in range(latents):
        part = slice(i * seq, (i + 1) * seq)
        pre = nn(u2_ref[part], up_ref[0]) + upb_ref[0]
        square = pre * pre
        bent = jnp.tanh(GELU_SCALE * (pre + GELU_CUBE * (square * pre)))
        half = 0.5 * (1.0 + bent)
        act = (pre * half).astype(low_type)
        g_ref[0, part] = act
        slope_ref[0, part] = (
            half
            + (0.5 * GELU_SCALE)
            * pre
            * (1.0 - bent * bent)
            * (1.0 + (3.0 * GELU_CUBE) * square)
        ).astype(low_type)
        part_sum = nn(act, down_ref[0])

        @pl.when(step == 0)
        def _():
            m_ref[part] = part_sum + downb_ref[...]

        @pl.when(step > 0)
        def _():
            m_ref[part] = m_ref[part] + part_sum

        @pl.when(step == pl.num_programs(0) - 1)
        def _():
            x_ref[part] = x1_ref[part] + mod_ref[i, 5:6] * m_ref[part]


def feed_back_kernel(
    dy_ref, m_ref, mod_ref, u2_ref, g_ref, slope_ref, up_ref, down_ref,
    gw_ref, du_ref, dgate_ref, downb_ref, upb_ref, dm_ref, df_ref,
):
    latents = mod_ref.shape[0]
    seq = u2_ref.shape[0] // latents
    step = pl.program_id(0)

    @pl.when(step == 0)
    def _():
        total = jnp.zeros(downb_ref.shape, wide)
        for i in range(latents):
            part = slice(i * seq, (i + 1) * seq)
            grad = dy_ref[part]
            dgate_ref[i] = jnp.sum(grad * m_ref[part], axis=0, keepdims=True)
            lower = (grad * mod_ref[i, 5:6]).astype(low_type)
            dm_ref[part] = lower
            total += jnp.sum(lower.astype(wide), axis=0, keepdims=True)
        downb_ref[...] = total

    sums = jnp.zeros(upb_ref.shape[1:], wide)
    for i in range(latents):
        part = slice(i * seq, (i + 1) * seq)
        lower = (nt(dm_ref[part], down_ref[0]) * slope_ref[0, part].astype(wide)).astype(low_type)
        df_ref[part] = lower
        sums += jnp.sum(lower.astype(wide), axis=0, keepdims=True)
        back = nt(lower, up_ref[0])

        @pl.when(step == 0)
        def _():
            du_ref[part] = back

        @pl.when(step > 0)
        def _():
            du_ref[part] = du_ref[part] + back

    upb_ref[0] = sums
    gw_ref[0, 0] = tn(g_ref[0], dm_ref[...]).astype(low_type)
    gw_ref[1, 0] = tn(u2_ref[...], df_ref[...]).astype(low_type)


def mix_back_kernel(
    du_ref, x1_ref, dy_ref, a_ref, qkv_ref, mod_ref, w_ref,
    dx1_ref, dall_ref, dmod_ref, sums_ref, do_ref,
):
    seq, width = x1_ref.shape
    pair = 2 * HEAD_DIM
    back, dshift, dscale = norm_back(du_ref[...], x1_ref[...], mod_ref[0, 4:5])
    dx1 = back + dy_ref[...]
    dx1_ref[...] = dx1
    dmod_ref[0, 0:1] = dshift
    dmod_ref[0, 1:2] = dscale
    dmod_ref[0, 2:3] = jnp.sum(dx1 * a_ref[...], axis=0, keepdims=True)
    da = (dx1 * mod_ref[0, 2:3]).astype(low_type)
    dall_ref[3] = da
    do_ref[...] = nt(da, w_ref[0]).astype(low_type)
    lane = lax.broadcasted_iota(jnp.int32, (seq, pair), 1)
    left = lane < HEAD_DIM
    for at in range(0, width, pair):
        cols = slice(at, at + pair)
        query = qkv_ref[0, :, cols]
        key = qkv_ref[1, :, cols]
        value = qkv_ref[2, :, cols]
        grad = do_ref[:, cols]
        found = []
        for side in (left, jnp.logical_not(left)):
            none = jnp.zeros_like(query)
            raw = nt(key, jnp.where(side, query, none)) * HEAD_DIM ** (-0.5)
            top = jnp.exp(raw - jnp.max(raw, axis=0, keepdims=True))
            probs = top * (1.0 / jnp.sum(top, axis=0, keepdims=True))
            dvalue = nn(probs.astype(low_type), grad)
            dprobs = nt(value, jnp.where(side, grad, none))
            dots = jnp.sum(dprobs * probs, axis=0, keepdims=True)
            draw = (probs * (dprobs - dots) * HEAD_DIM ** (-0.5)).astype(low_type)
            found.append((tn(draw, key), nn(draw, query), dvalue))
        for which in range(3):
            dall_ref[which, :, cols] = jnp.where(
                left, found[0][which], found[1][which]
            ).astype(low_type)

    @pl.when(pl.program_id(0) == 0)
    def _():
        sums_ref[...] = jnp.zeros_like(sums_ref)

    for which in range(4):
        sums_ref[which : which + 1] += jnp.sum(
            dall_ref[which].astype(wide), axis=0, keepdims=True
        )


def qkv_back_kernel(
    u1_ref, o_ref, dall_ref, w_ref, x_ref, dx1_ref, mod_ref, gw_ref, dx_ref, dmod_ref, acc_ref
):
    latents, seq, _ = x_ref.shape
    step = pl.program_id(0)

    @pl.when(step < 3)
    def _():
        gw_ref[0] = tn(u1_ref[...], dall_ref[0]).astype(low_type)
        for i in range(latents):
            part = slice(i * seq, (i + 1) * seq)
            back = nt(dall_ref[0, part], w_ref[0])

            @pl.when(step == 0)
            def _():
                acc_ref[part] = back

            @pl.when(step > 0)
            def _():
                acc_ref[part] = acc_ref[part] + back

    @pl.when(step == 3)
    def _():
        gw_ref[0] = tn(o_ref[...], dall_ref[0]).astype(low_type)
        for i in range(latents):
            part = slice(i * seq, (i + 1) * seq)
            back, dshift, dscale = norm_back(acc_ref[part], x_ref[i], mod_ref[i, 1:2])
            dx_ref[i] = back + dx1_ref[part]
            dmod_ref[i, 0:1] = dshift
            dmod_ref[i, 1:2] = dscale


def shape_of(dims, kind):
    return jax.ShapeDtypeStruct(tuple(dims), kind)


def full(dims):
    return pl.BlockSpec(tuple(dims), lambda step: (0,) * len(dims))


def along(dims, where):
    return pl.BlockSpec(
        tuple(dims), lambda step: tuple(step if i == where else 0 for i in range(len(dims)))
    )


def call(kernel, grid, in_specs, out_specs, out_shape, scratch, flops, moved):
    return pl.pallas_call(
        kernel,
        grid=(grid,),
        in_specs=in_specs,
        out_specs=out_specs,
        out_shape=out_shape,
        scratch_shapes=scratch,
        compiler_params=pltpu.CompilerParams(vmem_limit_bytes=56 * 2**20),
        cost_estimate=pl.CostEstimate(flops=flops, bytes_accessed=moved, transcendentals=0),
        name=kernel.__name__,
    )


def forward_layer(hidden, mod, weights):
    attn_w, up_w, down_w, qkv_b, proj_b, up_b, down_b = weights
    latents, seq, width = hidden.shape
    rows = latents * seq
    unit = 2 * rows * width * width
    size = rows * width
    u1, qkv = call(
        qkv_kernel,
        3,
        [
            full(hidden.shape),
            full(mod.shape),
            along((1, width, width), 0),
            along((1, 1, width), 0),
        ],
        [full((rows, width)), along((1, rows, width), 0)],
        [shape_of((rows, width), low_type), shape_of((3, rows, width), low_type)],
        [],
        3 * unit,
        18 * size,
    )(hidden, mod, attn_w, qkv_b)
    token = along((seq, width), 0)
    mixed, branch, middle, u2 = call(
        mix_kernel,
        latents,
        [
            along((3, seq, width), 1),
            along((1, seq, width), 0),
            along((1, 6, width), 0),
            pl.BlockSpec((1, width, width), lambda step: (3, 0, 0)),
            full((1, width)),
        ],
        [token, token, token, token],
        [
            shape_of((rows, width), low_type),
            shape_of((rows, width), wide),
            shape_of((rows, width), wide),
            shape_of((rows, width), low_type),
        ],
        [],
        5 * unit,
        24 * size,
    )(qkv, hidden, mod, attn_w, proj_b)
    act, slope, branch_two, result = call(
        feed_kernel,
        SLABS,
        [
            full((rows, width)),
            full((rows, width)),
            full(mod.shape),
            along((1, width, width), 0),
            along((1, 1, width), 0),
            along((1, width, width), 0),
            full((1, width)),
        ],
        [
            along((1, rows, width), 0),
            along((1, rows, width), 0),
            full((rows, width)),
            full((rows, width)),
        ],
        [
            shape_of((SLABS, rows, width), low_type),
            shape_of((SLABS, rows, width), low_type),
            shape_of((rows, width), wide),
            shape_of((rows, width), wide),
        ],
        [],
        12 * unit,
        40 * size,
    )(u2, middle, mod, up_w, up_b, down_w, down_b)
    saved = (hidden, mod, u1, qkv, mixed, branch, middle, u2, act, slope, branch_two)
    return result.reshape(hidden.shape), saved


def backward_layer(grad_out, weights, saved):
    attn_w, up_w, down_w = weights[:3]
    hidden, mod, u1, qkv, mixed, branch, middle, u2, act, slope, branch_two = saved
    latents, seq, width = hidden.shape
    rows = latents * seq
    unit = 2 * rows * width * width
    size = rows * width
    grad_out = grad_out.reshape(rows, width)
    block = along((1, rows, width), 0)
    square = along((1, width, width), 0)
    flat = full((rows, width))
    ff_grads, du2, dgate_two, down_sums, up_sums = call(
        feed_back_kernel,
        SLABS,
        [flat, flat, full(mod.shape), flat, block, block, square, square],
        [
            along((2, 1, width, width), 1),
            flat,
            full((latents, 1, width)),
            full((1, width)),
            along((1, 1, width), 0),
        ],
        [
            shape_of((2, SLABS, width, width), low_type),
            shape_of((rows, width), wide),
            shape_of((latents, 1, width), wide),
            shape_of((1, width), wide),
            shape_of((SLABS, 1, width), wide),
        ],
        [pltpu.VMEM((rows, width), low_type), pltpu.VMEM((rows, width), low_type)],
        16 * unit,
        50 * size,
    )(grad_out, branch_two, mod, u2, act, slope, up_w, down_w)
    token = along((seq, width), 0)
    dx1, dall, dmod_mid, sums = call(
        mix_back_kernel,
        latents,
        [
            token,
            token,
            token,
            token,
            along((3, seq, width), 1),
            along((1, 6, width), 0),
            pl.BlockSpec((1, width, width), lambda step: (3, 0, 0)),
        ],
        [
            token,
            along((4, seq, width), 1),
            along((1, 3, width), 0),
            full((4, width)),
        ],
        [
            shape_of((rows, width), wide),
            shape_of((4, rows, width), low_type),
            shape_of((latents, 3, width), wide),
            shape_of((4, width), wide),
        ],
        [pltpu.VMEM((seq, width), low_type)],
        10 * unit,
        40 * size,
    )(du2, middle, grad_out, branch, qkv, mod, attn_w)
    at_grads, dx, dmod_low = call(
        qkv_back_kernel,
        4,
        [
            flat,
            flat,
            block,
            square,
            full(hidden.shape),
            flat,
            full(mod.shape),
        ],
        [square, full(hidden.shape), full((latents, 2, width))],
        [
            shape_of((4, width, width), low_type),
            shape_of(hidden.shape, wide),
            shape_of((latents, 2, width), wide),
        ],
        [pltpu.VMEM((rows, width), wide)],
        7 * unit,
        36 * size,
    )(u1, mixed, dall, attn_w, hidden, dx1, mod)
    dmod = jnp.concatenate(
        [dmod_low, dmod_mid[:, 2:3], dmod_mid[:, 0:2], dgate_two], axis=1
    ).reshape(latents, 6 * width)
    return dx, dmod, ff_grads, at_grads, (sums, up_sums, down_sums)


class Net:
    def __init__(self, mesh):
        self.replicas = mesh.shape["replica"]
        self.shards = mesh.shape["shard"]

    def swap(self, values, axis, step):
        count = self.replicas if axis == "replica" else self.shards
        return lax.ppermute(values, axis, [(i, i ^ step) for i in range(count)])

    def bits(self, axis):
        count = self.replicas if axis == "replica" else self.shards
        found = []
        step = 1
        while step < count:
            found.append(step)
            step *= 2
        return found

    def gather_rel(self, values, axes):
        stack = values[None]
        for axis in axes:
            for step in self.bits(axis):
                stack = jnp.concatenate([stack, self.swap(stack, axis, step)])
        return stack

    def scatter_rel(self, stack):
        for step in self.bits("shard"):
            pairs = stack.reshape((stack.shape[0] // 2, 2) + stack.shape[1:])
            stack = pairs[:, 0] + self.swap(pairs[:, 1], "shard", 1 * step)
        return stack[0]


def order_kernel(places, pieces_per_slab, here_ref, near_ref, keep_ref, send_ref):
    shard_low = here_ref[0] % 2
    replica = here_ref[1]
    for place in range(places):
        piece = jnp.bitwise_xor(replica, place)
        slab = piece // pieces_per_slab
        part = piece % pieces_per_slab
        keep_ref[0, place] = near_ref[slab, shard_low, part].astype(keep_ref.dtype)
        send_ref[0, place] = near_ref[slab, 1 - shard_low, part].astype(send_ref.dtype)


def order_grads(net, here, grads):
    slabs, shards, rows, width = grads.shape
    per_slab = net.replicas // SLABS if net.replicas > SLABS else 1
    places = net.replicas
    if net.replicas < SLABS:
        raise ValueError("replicas")
    piece_rows = rows * SLABS // places
    groups = slabs // SLABS
    view = grads.reshape(groups, SLABS, shards, per_slab, piece_rows, width)
    out = jax.ShapeDtypeStruct((groups, shards // 2, places, piece_rows, width), low_type)
    spec = pl.BlockSpec(
        (None, 1, places, piece_rows, width), lambda g, j, here_ref: (g, j, 0, 0, 0)
    )
    return pl.pallas_call(
        functools.partial(order_kernel, places, per_slab),
        grid_spec=pltpu.PrefetchScalarGridSpec(
            num_scalar_prefetch=1,
            grid=(groups, shards // 2),
            in_specs=[
                pl.BlockSpec(
                    (None, SLABS, 2, per_slab, piece_rows, width),
                    lambda g, j, here_ref: (
                        g,
                        0,
                        jnp.bitwise_xor(here_ref[0] // 2, j),
                        0,
                        0,
                        0,
                    ),
                )
            ],
            out_specs=[spec, spec],
        ),
        out_shape=[out, out],
        name="order_grads",
    )(here, view)


def add_low(left, right):
    return (left.astype(wide) + right.astype(wide)).astype(low_type)


def halve(stack, dim, where):
    size = stack.shape[dim]
    shape = stack.shape[:dim] + (size // (2 * where), 2, where) + stack.shape[dim + 1 :]
    view = stack.reshape(shape)
    rest = stack.shape[:dim] + (size // 2,) + stack.shape[dim + 1 :]
    return (
        lax.index_in_dim(view, 0, dim + 1, keepdims=False).reshape(rest),
        lax.index_in_dim(view, 1, dim + 1, keepdims=False).reshape(rest),
    )


def reduce_grads(net, here, grads):
    keep, give = order_grads(net, here, grads)
    total = add_low(keep, net.swap(give, "shard", 1))
    groups, near, places, rows, width = total.shape
    done = []
    for part, order in ((0, 1), (1, -1)):
        piece = total[:, :, :, part * (rows // 2) : (part + 1) * (rows // 2)]
        left = list(range(places))
        for step in net.bits("replica")[::order]:
            where = sum(1 for q in left if q < step)
            keep, give = halve(piece, 2, where)
            left = [q for q in left if not q & step]
            piece = add_low(keep, net.swap(give, "replica", step))
        done.append(piece[:, :, 0])
    total = jnp.concatenate(done, axis=2)
    for step in net.bits("shard")[1:]:
        keep, give = halve(total, 1, 1)
        total = add_low(keep, net.swap(give, "shard", step))
    mine = total[:, 0]
    every = [mine] + [net.swap(mine, "replica", step) for step in range(1, places)]
    stack = jnp.stack(every)
    own = jnp.arange(places, dtype=jnp.int32)
    return jnp.take(stack, jnp.bitwise_xor(own, here[1]), axis=0).astype(wide)


def local(
    net,
    hidden_in,
    condition,
    latent_live,
    out_grad,
    ada_weight,
    qkv_weight,
    proj_weight,
    fc1_weight,
    fc2_weight,
    ada_bias,
    qv_bias,
    proj_bias,
    fc1_bias,
    fc2_bias,
):
    shard = lax.axis_index("shard")
    replica = lax.axis_index("replica")
    here = jnp.stack([shard, replica]).astype(jnp.int32)
    shards, replicas = net.shards, net.replicas
    latents_here, model_width = condition.shape
    rows = proj_weight.shape[1]
    piece_rows = rows * SLABS // replicas
    mod_width = ada_weight.shape[2]

    def pack(layer):
        qkv = qkv_weight[layer].astype(low_type)
        up = fc1_weight[layer].astype(low_type)
        up = up.reshape(rows, shards, SLABS, rows).transpose(2, 0, 1, 3)
        down = fc2_weight[layer].astype(low_type)
        blocks = [qkv[:, b * model_width : (b + 1) * model_width] for b in range(3)]
        blocks += [proj_weight[layer].astype(low_type)]
        blocks += [up[b].reshape(rows, model_width) for b in range(SLABS)]
        blocks += [down[b * rows : (b + 1) * rows] for b in range(SLABS)]
        packed = jnp.stack(blocks).reshape(3, replicas, piece_rows, model_width)
        return lax.dynamic_index_in_dim(packed, replica, 1, keepdims=False)

    gathered = []
    for layer in range(LAYERS):
        whole = lax.all_gather(pack(layer), ("replica", "shard"), axis=0, tiled=False)
        whole = whole.reshape(
            SLABS, replicas // SLABS, shards, 3, piece_rows, model_width
        ).transpose(3, 0, 2, 1, 4, 5)
        gathered.append(whole.reshape(3, SLABS, shards, rows, model_width))

    cond_low = jax.nn.silu(condition).astype(low_type)
    bias_rows = jnp.concatenate([qv_bias, proj_bias, fc1_bias, fc2_bias], axis=1).astype(low_type)
    bias_width = bias_rows.shape[1]
    cond_rel = net.gather_rel(cond_low, ["shard"])
    bias_all = lax.all_gather(bias_rows, "shard", axis=0, tiled=False)
    cond_all_rel = net.gather_rel(cond_rel, ["replica"])
    group = shards * latents_here
    cond_rows = lax.dynamic_slice_in_dim(
        cond_rel.reshape(group, model_width), shard * rows, rows, axis=1
    )
    cond_every = lax.dynamic_slice_in_dim(
        cond_all_rel.reshape(replicas * group, model_width), shard * rows, rows, axis=1
    ).astype(wide)
    ada_low = ada_weight.astype(low_type)
    partial = jnp.stack([nn(cond_rows, ada_low[layer]) for layer in range(LAYERS)], axis=1)
    ada_part = ada_bias.shape[1]
    bias_here = lax.dynamic_update_slice_in_dim(
        jnp.zeros((LAYERS, mod_width), wide),
        ada_bias.astype(low_type).astype(wide),
        shard * ada_part,
        axis=1,
    )
    partial = (partial + bias_here[None]).reshape(shards, latents_here, LAYERS, mod_width)
    modulations = net.scatter_rel(partial)

    widths = (qv_bias.shape[1], proj_bias.shape[1], fc1_bias.shape[1], fc2_bias.shape[1])
    starts = (0, widths[0], widths[0] + widths[1], widths[0] + widths[1] + widths[2])

    def weights_of(layer):
        slabs = gathered[layer].reshape(3, SLABS, model_width, model_width)
        qv, proj, up, down = [
            bias_all[:, layer, start : start + width].reshape(-1).astype(wide)
            for start, width in zip(starts, widths)
        ]
        qkv_b = jnp.stack([qv[:model_width], jnp.zeros((model_width,), wide), qv[model_width:]])
        up_b = up.reshape(shards, SLABS, rows).transpose(1, 0, 2).reshape(SLABS, 1, model_width)
        return (
            slabs[0],
            slabs[1],
            slabs[2],
            qkv_b[:, None],
            proj[None],
            up_b,
            down[None],
        )

    live_rows = latent_live.astype(wide)[:, None, None]
    saved_all = []
    current = hidden_in
    weights_all = [weights_of(layer) for layer in range(LAYERS)]
    for layer in range(LAYERS):
        current, saved_state = forward_layer(
            current, modulations[:, layer].reshape(latents_here, 6, model_width), weights_all[layer]
        )
        saved_all.append(saved_state)
    result = current * live_rows
    grad_now = out_grad * live_rows

    def send(grads):
        slabs = grads.reshape(-1, shards, rows, model_width)
        return reduce_grads(net, here, slabs)

    ada_wide = ada_low.astype(wide)
    grad_cond = jnp.zeros((group, rows), wide)
    owned = [None] * LAYERS
    ada_grads = [None] * LAYERS
    ada_bias_grads = [None] * LAYERS
    bias_sums = [None] * LAYERS
    for layer in reversed(range(LAYERS)):
        grad_now, grad_modul, ff_grads, at_grads, (sums, up_sums, down_sums) = backward_layer(
            grad_now, weights_all[layer], saved_all[layer]
        )
        ff_owned = send(ff_grads)
        at_owned = send(at_grads)
        bias_grads = (
            jnp.concatenate([sums[0], sums[2]]),
            sums[3],
            up_sums.reshape(SLABS, shards, rows).transpose(1, 0, 2).reshape(-1),
            down_sums[0],
        )
        modul_rel = net.gather_rel(net.gather_rel(grad_modul, ["shard"]), ["replica"])
        modul_rel = modul_rel.reshape(replicas, group, mod_width)
        grad_cond = grad_cond + exact_trail(modul_rel[0], ada_wide[layer])
        modul_every = modul_rel.reshape(replicas * group, mod_width)
        ada_grads[layer] = exact_lead(cond_every, modul_every)
        ada_bias_grads[layer] = jnp.sum(
            lax.dynamic_slice_in_dim(modul_every, shard * ada_part, ada_part, axis=1), axis=0
        )
        at_rows = at_owned.transpose(1, 0, 2, 3).reshape(SLABS, rows, model_width)
        ff_rows = ff_owned.transpose(1, 0, 2, 3).reshape(2, SLABS, rows, model_width)
        wide_of = lambda w: w.transpose(1, 0, 2).reshape(rows, -1)
        owned[layer] = (
            wide_of(at_rows[:3]),
            at_rows[3],
            ff_rows[1]
            .reshape(SLABS, rows, shards, rows)
            .transpose(1, 2, 0, 3)
            .reshape(rows, SLABS * model_width),
            ff_rows[0].reshape(SLABS * rows, model_width),
        )
        bias_sums[layer] = jnp.concatenate(
            [grad.reshape(shards, -1) for grad in bias_grads], axis=1
        )
    bias_total = lax.psum(jnp.stack(bias_sums), ("replica", "shard"))
    bias_mine = lax.dynamic_index_in_dim(bias_total, shard, 1, keepdims=False)
    bias_out = [bias_mine[:, start : start + width] for start, width in zip(starts, widths)]

    parts = grad_cond.reshape(shards, latents_here, rows)
    back = [parts[0]] + [net.swap(parts[step], "shard", step) for step in range(1, shards)]
    back = jnp.take(
        jnp.stack(back), jnp.bitwise_xor(jnp.arange(shards, dtype=jnp.int32), here[0]), axis=0
    )
    cond_back = back.transpose(1, 0, 2).reshape(latents_here, model_width)
    grad_condition = jax.vjp(jax.nn.silu, condition)[1](cond_back)[0]
    return (
        result,
        grad_now,
        grad_condition,
        jnp.stack(ada_grads),
        jnp.stack([owned[layer][0] for layer in range(LAYERS)]),
        jnp.stack([owned[layer][1] for layer in range(LAYERS)]),
        jnp.stack([owned[layer][2] for layer in range(LAYERS)]),
        jnp.stack([owned[layer][3] for layer in range(LAYERS)]),
        jnp.stack(ada_bias_grads),
        *bias_out,
    )


def solution(mesh):
    tokens = P(("replica", "shard"), None, None)
    weight = P(None, "shard", None)
    bias = P(None, "shard")
    rows = P(("replica", "shard"), None)
    return jax.shard_map(
        functools.partial(local, Net(mesh)),
        mesh=mesh,
        in_specs=(tokens, rows, P(("replica", "shard")), tokens) + (weight,) * 5 + (bias,) * 5,
        out_specs=(tokens, tokens, rows) + (weight,) * 5 + (bias,) * 5,
        check_vma=False,
    )
```

```python
import functools

import jax
import jax.numpy as jnp
from jax import lax
from jax.experimental import pallas as pl
from jax.experimental.pallas import tpu as pltpu
from jax.sharding import PartitionSpec as P

HEADS = 12
HEAD_DIM = 64
LAYERS = 2
SLABS = 4

norm_eps = 1e-06
highest = lax.Precision.HIGHEST
low_type = jnp.bfloat16
wide = jnp.float32


def nn(left, right):
    return lax.dot_general(left, right, (((1,), (0,)), ((), ())), preferred_element_type=wide)


def nt(left, right):
    return lax.dot_general(left, right, (((1,), (1,)), ((), ())), preferred_element_type=wide)


def tn(left, right):
    return lax.dot_general(left, right, (((0,), (0,)), ((), ())), preferred_element_type=wide)


def exact_lead(left_side, right_side):
    return lax.dot_general(
        left_side,
        right_side,
        (((0,), (0,)), ((), ())),
        precision=highest,
        preferred_element_type=wide,
    )


def exact_trail(left_side, right_side):
    return lax.dot_general(
        left_side,
        right_side,
        (((1,), (1,)), ((), ())),
        precision=highest,
        preferred_element_type=wide,
    )


def normalise(rows):
    centred = rows - jnp.mean(rows, axis=-1, keepdims=True)
    spread = jnp.mean(centred * centred, axis=-1, keepdims=True)
    inverse = lax.rsqrt(spread + norm_eps)
    return centred * inverse, inverse


def norm_back(grad, rows, stretch):
    normed, inverse = normalise(rows)
    inner = grad * (1.0 + stretch)
    first = jnp.mean(inner, axis=-1, keepdims=True)
    second = jnp.mean(inner * normed, axis=-1, keepdims=True)
    back = (inner - first - normed * second) * inverse
    return (
        back,
        jnp.sum(grad, axis=0, keepdims=True),
        jnp.sum(grad * normed, axis=0, keepdims=True),
    )


def slab(ref):
    return ref[0].reshape(ref.shape[3], ref.shape[3])


def tall(ref):
    if ref.shape[0] == 1:
        return slab(ref)
    return jnp.concatenate(
        [ref[r, s] for s in range(ref.shape[1]) for r in range(ref.shape[0])], axis=0
    )


def qkv_kernel(x_ref, mod_ref, w_ref, b_ref, u_ref, qkv_ref):
    latents, seq, _ = x_ref.shape

    @pl.when(pl.program_id(0) == 0)
    def _():
        for i in range(latents):
            normed, _ = normalise(x_ref[i])
            u_ref[i * seq : (i + 1) * seq] = (
                normed * (1.0 + mod_ref[i, 1:2]) + mod_ref[i, 0:1]
            ).astype(low_type)

    for i in range(latents):
        part = slice(i * seq, (i + 1) * seq)
        qkv_ref[0, part] = (nn(u_ref[part], slab(w_ref)) + b_ref[0]).astype(low_type)


def mix_kernel(qkv_ref, x_ref, mod_ref, w_ref, b_ref, o_ref, a_ref, x1_ref, u2_ref):
    seq, width = o_ref.shape
    pair = 2 * HEAD_DIM
    lane = lax.broadcasted_iota(jnp.int32, (seq, pair), 1)
    left = lane < HEAD_DIM
    for at in range(0, width, pair):
        query = qkv_ref[0, :, at : at + pair]
        key = qkv_ref[1, :, at : at + pair]
        value = qkv_ref[2, :, at : at + pair]
        mixed = []
        for side in (left, jnp.logical_not(left)):
            raw = nt(jnp.where(side, query, jnp.zeros_like(query)), key) * HEAD_DIM ** (-0.5)
            top = jnp.exp(raw - jnp.max(raw, axis=-1, keepdims=True))
            probs = top * (1.0 / jnp.sum(top, axis=-1, keepdims=True))
            mixed.append(nn(probs.astype(low_type), value))
        o_ref[:, at : at + pair] = jnp.where(left, mixed[0], mixed[1]).astype(low_type)
    branch = nn(o_ref[...], slab(w_ref)) + b_ref[...]
    a_ref[...] = branch
    middle = x_ref[0] + mod_ref[0, 2:3] * branch
    x1_ref[...] = middle
    normed, _ = normalise(middle)
    u2_ref[...] = (normed * (1.0 + mod_ref[0, 4:5]) + mod_ref[0, 3:4]).astype(low_type)


GELU_SCALE = 0.7978845608028654
GELU_CUBE = 0.044715


def feed_kernel(
    u2_ref, x1_ref, mod_ref, up_ref, upb_ref, down_ref, downb_ref, g_ref, slope_ref, m_ref, x_ref
):
    latents = mod_ref.shape[0]
    seq = u2_ref.shape[0] // latents
    step = pl.program_id(0)
    down = tall(down_ref)
    for i in range(latents):
        part = slice(i * seq, (i + 1) * seq)
        pre = nn(u2_ref[part], slab(up_ref)) + upb_ref[0]
        square = pre * pre
        bent = jnp.tanh(GELU_SCALE * (pre + GELU_CUBE * (square * pre)))
        half = 0.5 * (1.0 + bent)
        act = (pre * half).astype(low_type)
        g_ref[0, part] = act
        slope_ref[0, part] = (
            half
            + (0.5 * GELU_SCALE)
            * pre
            * (1.0 - bent * bent)
            * (1.0 + (3.0 * GELU_CUBE) * square)
        ).astype(low_type)
        part_sum = nn(act, down)

        @pl.when(step == 0)
        def _():
            m_ref[part] = part_sum + downb_ref[...]

        @pl.when(step > 0)
        def _():
            m_ref[part] = m_ref[part] + part_sum

        @pl.when(step == pl.num_programs(0) - 1)
        def _():
            x_ref[part] = x1_ref[part] + mod_ref[i, 5:6] * m_ref[part]


def store_slab(here_ref, product, kept_ref, sent_ref, hold_ref):
    hold_ref[...] = product.astype(low_type).reshape(hold_ref.shape)
    for near in range(kept_ref.shape[0]):
        owner = jnp.bitwise_xor(here_ref[0], 2 * near)
        kept_ref[near, 0] = hold_ref[owner]
        sent_ref[near, 0] = hold_ref[jnp.bitwise_xor(owner, 1)]


def feed_back_kernel(
    fused, here_ref, dy_ref, m_ref, mod_ref, u2_ref, g_ref, slope_ref, up_ref, down_ref,
    *refs,
):
    if fused:
        up_grads, down_grads, refs = refs[:2], refs[2:4], refs[4:]
    else:
        up_grad, down_grad, refs = refs[0], refs[1], refs[2:]
    du_ref, dgate_ref, downb_ref, upb_ref, dm_ref, df_ref, hold_ref = refs
    latents = mod_ref.shape[0]
    seq = u2_ref.shape[0] // latents
    step = pl.program_id(0)

    @pl.when(step == 0)
    def _():
        total = jnp.zeros(downb_ref.shape, wide)
        for i in range(latents):
            part = slice(i * seq, (i + 1) * seq)
            grad = dy_ref[part]
            dgate_ref[i] = jnp.sum(grad * m_ref[part], axis=0, keepdims=True)
            lower = (grad * mod_ref[i, 5:6]).astype(low_type)
            dm_ref[part] = lower
            total += jnp.sum(lower.astype(wide), axis=0, keepdims=True)
        downb_ref[...] = total

    sums = jnp.zeros(upb_ref.shape[1:], wide)
    down = tall(down_ref)
    for i in range(latents):
        part = slice(i * seq, (i + 1) * seq)
        lower = (nt(dm_ref[part], down) * slope_ref[0, part].astype(wide)).astype(low_type)
        df_ref[part] = lower
        sums += jnp.sum(lower.astype(wide), axis=0, keepdims=True)
        back = nt(lower, slab(up_ref))

        @pl.when(step == 0)
        def _():
            du_ref[part] = back

        @pl.when(step > 0)
        def _():
            du_ref[part] = du_ref[part] + back

    upb_ref[0] = sums
    down_part = tn(g_ref[0], dm_ref[...])
    up_part = tn(u2_ref[...], df_ref[...])
    if not fused:
        down_grad[0] = down_part.astype(low_type)
        up_grad[0] = up_part.astype(low_type)
        return
    store_slab(here_ref, up_part, up_grads[0], up_grads[1], hold_ref)
    hold_ref[...] = down_part.astype(low_type).reshape(hold_ref.shape)
    places = down_grads[0].shape[1]
    low = here_ref[0] % 2
    for place in range(places):
        piece = jnp.bitwise_xor(here_ref[1], place)
        down_grads[0][0, place] = hold_ref[low * places + piece]
        down_grads[1][0, place] = hold_ref[(1 - low) * places + piece]


def mix_back_kernel(
    du_ref, x1_ref, dy_ref, a_ref, qkv_ref, mod_ref, w_ref,
    dx1_ref, dall_ref, dmod_ref, sums_ref, do_ref,
):
    seq, width = x1_ref.shape
    pair = 2 * HEAD_DIM
    back, dshift, dscale = norm_back(du_ref[...], x1_ref[...], mod_ref[0, 4:5])
    dx1 = back + dy_ref[...]
    dx1_ref[...] = dx1
    dmod_ref[0, 0:1] = dshift
    dmod_ref[0, 1:2] = dscale
    dmod_ref[0, 2:3] = jnp.sum(dx1 * a_ref[...], axis=0, keepdims=True)
    da = (dx1 * mod_ref[0, 2:3]).astype(low_type)
    dall_ref[3] = da
    do_ref[...] = nt(da, slab(w_ref)).astype(low_type)
    lane = lax.broadcasted_iota(jnp.int32, (seq, pair), 1)
    left = lane < HEAD_DIM
    for at in range(0, width, pair):
        cols = slice(at, at + pair)
        query = qkv_ref[0, :, cols]
        key = qkv_ref[1, :, cols]
        value = qkv_ref[2, :, cols]
        grad = do_ref[:, cols]
        found = []
        for side in (left, jnp.logical_not(left)):
            none = jnp.zeros_like(query)
            raw = nt(key, jnp.where(side, query, none)) * HEAD_DIM ** (-0.5)
            top = jnp.exp(raw - jnp.max(raw, axis=0, keepdims=True))
            probs = top * (1.0 / jnp.sum(top, axis=0, keepdims=True))
            dvalue = nn(probs.astype(low_type), grad)
            dprobs = nt(value, jnp.where(side, grad, none))
            dots = jnp.sum(dprobs * probs, axis=0, keepdims=True)
            draw = (probs * (dprobs - dots) * HEAD_DIM ** (-0.5)).astype(low_type)
            found.append((tn(draw, key), nn(draw, query), dvalue))
        for which in range(3):
            dall_ref[which, :, cols] = jnp.where(
                left, found[0][which], found[1][which]
            ).astype(low_type)

    @pl.when(pl.program_id(0) == 0)
    def _():
        sums_ref[...] = jnp.zeros_like(sums_ref)

    for which in range(4):
        sums_ref[which : which + 1] += jnp.sum(
            dall_ref[which].astype(wide), axis=0, keepdims=True
        )


def qkv_back_kernel(
    fused, here_ref, u1_ref, o_ref, dall_ref, w_ref, x_ref, dx1_ref, mod_ref, *refs
):
    grads = refs[:2] if fused else refs[:1]
    dx_ref, dmod_ref, acc_ref, hold_ref = refs[len(grads) :]

    def store(product):
        if fused:
            store_slab(here_ref, product, grads[0], grads[1], hold_ref)
        else:
            grads[0][0] = product.astype(low_type)

    latents, seq, _ = x_ref.shape
    step = pl.program_id(0)

    @pl.when(step < 3)
    def _():
        store(tn(u1_ref[...], dall_ref[0]))
        for i in range(latents):
            part = slice(i * seq, (i + 1) * seq)
            back = nt(dall_ref[0, part], slab(w_ref))

            @pl.when(step == 0)
            def _():
                acc_ref[part] = back

            @pl.when(step > 0)
            def _():
                acc_ref[part] = acc_ref[part] + back

    @pl.when(step == 3)
    def _():
        store(tn(o_ref[...], dall_ref[0]))
        for i in range(latents):
            part = slice(i * seq, (i + 1) * seq)
            back, dshift, dscale = norm_back(acc_ref[part], x_ref[i], mod_ref[i, 1:2])
            dx_ref[i] = back + dx1_ref[part]
            dmod_ref[i, 0:1] = dshift
            dmod_ref[i, 1:2] = dscale


def shape_of(dims, kind):
    return jax.ShapeDtypeStruct(tuple(dims), kind)


def full(dims):
    return pl.BlockSpec(tuple(dims), lambda step, here_ref: (0,) * len(dims))


def along(dims, where):
    return pl.BlockSpec(
        tuple(dims),
        lambda step, here_ref: tuple(step if i == where else 0 for i in range(len(dims))),
    )


def slab_spec(weight, fixed=None):
    array, kind = weight
    _, shards, _, rows, width = array.shape
    return pl.BlockSpec(
        (1, shards, None, rows, width),
        lambda step, here_ref: (step if fixed is None else fixed, 0, kind, 0, 0),
    )


def tall_spec(weight):
    array, kind = weight
    slabs, shards, _, rows, width = array.shape
    if shards == 1:
        return slab_spec(weight)
    return pl.BlockSpec(
        (slabs, shards // slabs, None, rows, width), lambda step, here_ref: (0, step, kind, 0, 0)
    )


def call(
    kernel, here, grid, in_specs, out_specs, out_shape, scratch, flops, moved, after=(), fused=None
):
    count = len(in_specs)

    def body(here_ref, *refs):
        lead = () if fused is None else (fused, here_ref)
        kernel(*lead, *refs[:count], *refs[count + len(after) :])

    run = pl.pallas_call(
        body,
        grid_spec=pltpu.PrefetchScalarGridSpec(
            num_scalar_prefetch=1,
            grid=(grid,),
            in_specs=list(in_specs) + [pl.BlockSpec(memory_space=pl.ANY)] * len(after),
            out_specs=out_specs,
            scratch_shapes=scratch,
        ),
        out_shape=out_shape,
        compiler_params=pltpu.CompilerParams(vmem_limit_bytes=58 * 2**20),
        cost_estimate=pl.CostEstimate(flops=flops, bytes_accessed=moved, transcendentals=0),
        name=kernel.__name__,
    )
    return lambda *arrays: run(here, *arrays, *after)


def forward_layer(here, hidden, mod, attn, feed, biases, slots):
    qkv_b, proj_b, up_b, down_b = biases
    attn_w, after = attn()
    latents, seq, width = hidden.shape
    rows = latents * seq
    unit = 2 * rows * width * width
    size = rows * width
    u1, qkv = call(
        qkv_kernel,
        here,
        3,
        [
            full(hidden.shape),
            full(mod.shape),
            slab_spec(attn_w),
            along((1, 1, width), 0),
        ],
        [full((rows, width)), along((1, rows, width), 0)],
        [shape_of((rows, width), low_type), shape_of((3, rows, width), low_type)],
        [],
        3 * unit,
        18 * size,
        after,
    )(hidden, mod, attn_w[0], qkv_b)
    token = along((seq, width), 0)
    mixed, branch, middle, u2 = call(
        mix_kernel,
        here,
        latents,
        [
            along((3, seq, width), 1),
            along((1, seq, width), 0),
            along((1, 6, width), 0),
            slab_spec(attn_w, 3),
            full((1, width)),
        ],
        [token, token, token, token],
        [
            shape_of((rows, width), low_type),
            shape_of((rows, width), wide),
            shape_of((rows, width), wide),
            shape_of((rows, width), low_type),
        ],
        [],
        5 * unit,
        24 * size,
        slots(),
    )(qkv, hidden, mod, attn_w[0], proj_b)
    up_w, down_w, after = feed()
    act, slope, branch_two, result = call(
        feed_kernel,
        here,
        SLABS,
        [
            full((rows, width)),
            full((rows, width)),
            full(mod.shape),
            slab_spec(up_w),
            along((1, 1, width), 0),
            tall_spec(down_w),
            full((1, width)),
        ],
        [
            along((1, rows, width), 0),
            along((1, rows, width), 0),
            full((rows, width)),
            full((rows, width)),
        ],
        [
            shape_of((SLABS, rows, width), low_type),
            shape_of((SLABS, rows, width), low_type),
            shape_of((rows, width), wide),
            shape_of((rows, width), wide),
        ],
        [],
        12 * unit,
        40 * size,
        after,
    )(u2, middle, mod, up_w[0], up_b, down_w[0], down_b)
    saved = (hidden, mod, u1, qkv, mixed, branch, middle, u2, act, slope, branch_two)
    return result.reshape(hidden.shape), saved, (attn_w, up_w, down_w)


def backward_layer(here, fused, grad_out, weights, saved, before, middle_slot, late_slot):
    attn_w, up_w, down_w = weights
    hidden, mod, u1, qkv, mixed, branch, middle, u2, act, slope, branch_two = saved
    latents, seq, width = hidden.shape
    rows = latents * seq
    unit = 2 * rows * width * width
    size = rows * width
    grad_out = grad_out.reshape(rows, width)
    block = along((1, rows, width), 0)
    flat = full((rows, width))
    square = along((1, width, width), 0)
    _, shards, _, own, _ = attn_w[0].shape
    near = shards // 2
    by_place = pl.BlockSpec(
        (near, 1, own, width),
        lambda step, here_ref: (0, jnp.bitwise_xor(here_ref[1], step), 0, 0),
    )
    by_near = pl.BlockSpec(
        (1, SLABS, own, width),
        lambda step, here_ref: (jnp.bitwise_xor(here_ref[0] // 2, step), 0, 0, 0),
    )
    half = shape_of((near, SLABS, own, width), low_type)
    natural = shape_of((SLABS, width, width), low_type)
    hold = pltpu.VMEM((shards, own, width), low_type)
    *ff_grads, du2, dgate_two, down_sums, up_sums = call(
        feed_back_kernel,
        here,
        SLABS,
        [flat, flat, full(mod.shape), flat, block, block, slab_spec(up_w), tall_spec(down_w)],
        ([by_place, by_place, by_near, by_near] if fused else [square, square])
        + [flat, full((latents, 1, width)), full((1, width)), along((1, 1, width), 0)],
        ([half] * 4 if fused else [natural] * 2)
        + [
            shape_of((rows, width), wide),
            shape_of((latents, 1, width), wide),
            shape_of((1, width), wide),
            shape_of((SLABS, 1, width), wide),
        ],
        [pltpu.VMEM((rows, width), low_type), pltpu.VMEM((rows, width), low_type), hold],
        16 * unit,
        50 * size,
        before,
        fused,
    )(grad_out, branch_two, mod, u2, act, slope, up_w[0], down_w[0])
    token = along((seq, width), 0)
    dx1, dall, dmod_mid, sums = call(
        mix_back_kernel,
        here,
        latents,
        [
            token,
            token,
            token,
            token,
            along((3, seq, width), 1),
            along((1, 6, width), 0),
            slab_spec(attn_w, 3),
        ],
        [
            token,
            along((4, seq, width), 1),
            along((1, 3, width), 0),
            full((4, width)),
        ],
        [
            shape_of((rows, width), wide),
            shape_of((4, rows, width), low_type),
            shape_of((latents, 3, width), wide),
            shape_of((4, width), wide),
        ],
        [pltpu.VMEM((seq, width), low_type)],
        10 * unit,
        40 * size,
        middle_slot(ff_grads),
    )(du2, middle, grad_out, branch, qkv, mod, attn_w[0])
    *at_grads, dx, dmod_low = call(
        qkv_back_kernel,
        here,
        4,
        [flat, flat, block, slab_spec(attn_w), full(hidden.shape), flat, full(mod.shape)],
        ([by_place, by_place] if fused else [square])
        + [full(hidden.shape), full((latents, 2, width))],
        ([half] * 2 if fused else [natural])
        + [shape_of(hidden.shape, wide), shape_of((latents, 2, width), wide)],
        [pltpu.VMEM((rows, width), wide), hold],
        7 * unit,
        36 * size,
        late_slot(sums, up_sums, down_sums),
        fused,
    )(u1, mixed, dall, attn_w[0], hidden, dx1, mod)
    dmod = jnp.concatenate(
        [dmod_low, dmod_mid[:, 2:3], dmod_mid[:, 0:2], dgate_two], axis=1
    ).reshape(latents, 6 * width)
    return dx, dmod, at_grads


class Net:
    def __init__(self, mesh):
        self.replicas = mesh.shape["replica"]
        self.shards = mesh.shape["shard"]

    def swap(self, values, axis, step):
        count = self.replicas if axis == "replica" else self.shards
        return lax.ppermute(values, axis, [(i, i ^ step) for i in range(count)])

    def bits(self, axis):
        count = self.replicas if axis == "replica" else self.shards
        found = []
        step = 1
        while step < count:
            found.append(step)
            step *= 2
        return found

    def gather_rel(self, values, axes):
        stack = values[None]
        for axis in axes:
            for step in self.bits(axis)[::-1]:
                stack = jnp.concatenate([stack, self.swap(stack, axis, step)])
        return stack

    def gather_steps(self, values, axis):
        stack = values[None]
        for step in self.bits(axis)[::-1]:
            got = self.swap(stack, axis, step)
            yield [stack]
            stack = jnp.concatenate([stack, got])
        return stack

    def total_steps(self, values):
        for axis in ("shard", "replica"):
            for step in self.bits(axis):
                got = self.swap(values, axis, step)
                yield [values]
                values = values + got
        return values

    def order(self, axis):
        found = [0]
        for step in self.bits(axis)[::-1]:
            found = found + [place ^ step for place in found]
        return found

    def scatter_rel(self, stack):
        for step in self.bits("shard"):
            half = stack.shape[0] // 2
            stack = stack[:half] + self.swap(stack[half:], "shard", step)
        return stack[0]


def order_kernel(places, pieces_per_slab, here_ref, near_ref, keep_ref, send_ref):
    shard_low = here_ref[0] % 2
    replica = here_ref[1]
    for place in range(places):
        piece = jnp.bitwise_xor(replica, place)
        slab = piece // pieces_per_slab
        part = piece % pieces_per_slab
        keep_ref[0, place] = near_ref[slab, shard_low, part].astype(keep_ref.dtype)
        send_ref[0, place] = near_ref[slab, 1 - shard_low, part].astype(send_ref.dtype)


def order_grads(net, here, grads):
    slabs, shards, rows, width = grads.shape
    per_slab = net.replicas // SLABS if net.replicas > SLABS else 1
    places = net.replicas
    if net.replicas < SLABS:
        raise ValueError("replicas")
    piece_rows = rows * SLABS // places
    groups = slabs // SLABS
    view = grads.reshape(groups, SLABS, shards, per_slab, piece_rows, width)
    out = jax.ShapeDtypeStruct((groups, shards // 2, places, piece_rows, width), low_type)
    spec = pl.BlockSpec(
        (None, 1, places, piece_rows, width), lambda g, j, here_ref: (g, j, 0, 0, 0)
    )
    return pl.pallas_call(
        functools.partial(order_kernel, places, per_slab),
        grid_spec=pltpu.PrefetchScalarGridSpec(
            num_scalar_prefetch=1,
            grid=(groups, shards // 2),
            in_specs=[
                pl.BlockSpec(
                    (None, SLABS, 2, per_slab, piece_rows, width),
                    lambda g, j, here_ref: (
                        g,
                        0,
                        jnp.bitwise_xor(here_ref[0] // 2, j),
                        0,
                        0,
                        0,
                    ),
                )
            ],
            out_specs=[spec, spec],
        ),
        out_shape=[out, out],
        name="order_grads",
    )(here, view)


def add_low(left, right):
    return (left.astype(wide) + right.astype(wide)).astype(low_type)


def halve(stack, dim, where):
    size = stack.shape[dim]
    shape = stack.shape[:dim] + (size // (2 * where), 2, where) + stack.shape[dim + 1 :]
    view = stack.reshape(shape)
    rest = stack.shape[:dim] + (size // 2,) + stack.shape[dim + 1 :]
    return (
        lax.index_in_dim(view, 0, dim + 1, keepdims=False).reshape(rest),
        lax.index_in_dim(view, 1, dim + 1, keepdims=False).reshape(rest),
    )


def reduce_steps(net, here, pairs):
    gots = [net.swap(give, "shard", 1) for _, give in pairs]
    yield [give for _, give in pairs]
    near, places, rows, width = pairs[0][0].shape
    single = len(pairs) == 1
    if single:
        cuts = [slice(0, near // 2), slice(near // 2, near)]
        parts = [add_low(pairs[0][0][cut], gots[0][cut]) for cut in cuts]
    else:
        parts = [add_low(keep, got) for (keep, _), got in zip(pairs, gots)]
    lefts = [list(range(places))] * 2
    for steps in zip(net.bits("replica"), net.bits("replica")[::-1]):
        splits = []
        for i, step in enumerate(steps):
            where = sum(1 for q in lefts[i] if q < step)
            splits.append(halve(parts[i], 1, where))
            lefts[i] = [q for q in lefts[i] if not q & step]
        gots = [net.swap(give, "replica", step) for (_, give), step in zip(splits, steps)]
        yield [give for _, give in splits]
        parts = [add_low(keep, got) for (keep, _), got in zip(splits, gots)]
    parts = [part[:, 0] for part in parts]
    steps = net.bits("shard")[1:]
    for step in steps[:-1] if single else steps:
        splits = [halve(part, 0, 1) for part in parts]
        gots = [net.swap(give, "shard", step) for _, give in splits]
        yield [give for _, give in splits]
        parts = [add_low(keep, got) for (keep, _), got in zip(splits, gots)]
    if single:
        got = net.swap(parts[1], "shard", steps[-1])
        yield [parts[1]]
        mine = add_low(parts[0], got)
    else:
        mine = jnp.concatenate(parts)
    every = [mine] + [net.swap(mine, "replica", step) for step in range(1, places)]
    yield [mine]
    return every


class Part:
    def __init__(self, keep, labels, route):
        self.keep = keep
        self.got = None
        self.labels = labels
        self.route = route


class Fold:
    def __init__(self, net, pairs):
        self.net = net
        near, places, rows, width = pairs[0][0].shape
        ahead = [("replica", step) for step in net.bits("replica")]
        behind = ahead[::-1]
        shard_route = [("shard", step) for step in net.bits("shard")[1:]]
        flat = (near * places, rows, width)
        keeps = [keep.reshape(flat) for keep, _ in pairs]
        gives = [give.reshape(flat) for _, give in pairs]
        self.gots = [net.swap(give, "shard", 1) for give in gives]
        self.sent = gives
        labels = [(2 * t, q) for t in range(near) for q in range(places)]
        self.single = len(pairs) == 1
        if self.single:
            half = len(labels) // 2
            self.parts = [
                Part((keeps[0], 0), labels[:half], ahead + shard_route[:-1]),
                Part((keeps[0], half), labels[half:], behind + shard_route[:-1]),
            ]
            self.last = shard_route[-1]
            for part, start in zip(self.parts, (0, half)):
                part.got = (self.gots[0], start)
        else:
            self.parts = [
                Part((keeps[0], 0), labels, ahead + shard_route),
                Part((keeps[1], 0), labels, behind + shard_route),
            ]
            for part, got in zip(self.parts, self.gots):
                part.got = (got, 0)
        self.every = None
        self.merge = False

    def jobs(self):
        if self.every is not None:
            return [], []
        first = self.parts[0]
        rows, width = first.keep[0].shape[1:]
        if self.merge or not first.route:
            if self.single and not self.merge:
                a, b = self.parts
                return [(a, [0], 0), (b, [0], 1)], [(1, rows, width)] * 2
            parts = self.parts[:1] if self.single else self.parts
            jobs = [(part, [0], 0) for part in parts]
            return jobs, [(len(parts), rows, width)]
        jobs, outs = [], []
        for part in self.parts:
            axis, step = part.route[0]
            which = 0 if axis == "shard" else 1
            stay = [i for i, label in enumerate(part.labels) if not label[which] & step]
            leave = [i for i, label in enumerate(part.labels) if label[which] & step]
            for blocks in (stay, leave):
                jobs.append((part, blocks, len(outs)))
                outs.append((len(blocks), rows, width))
        return jobs, outs

    def take(self, outs):
        if self.every is not None:
            return []
        net = self.net
        if self.merge or not self.parts[0].route:
            if self.single and not self.merge:
                self.merge = True
                axis, step = self.last
                self.parts[0].keep = (outs[0], 0)
                self.parts[0].got = (net.swap(outs[1], axis, step), 0)
                return [outs[1]]
            mine = outs[0]
            self.every = [mine]
            self.every += [net.swap(mine, "replica", step) for step in range(1, net.replicas)]
            return [mine]
        sent = []
        for part, (keep, give) in zip(self.parts, zip(outs[::2], outs[1::2])):
            (axis, step), part.route = part.route[0], part.route[1:]
            which = 0 if axis == "shard" else 1
            part.labels = [label for label in part.labels if not label[which] & step]
            part.keep = (keep, 0)
            part.got = (net.swap(give, axis, step), 0)
            sent.append(give)
        return sent


def round_kernel(jobs, *refs):
    place = [0] * 64
    for keep, got, blocks, keep_at, got_at, out in jobs:
        for block in blocks:
            refs[out][place[out]] = (
                refs[keep][keep_at + block].astype(wide) + refs[got][got_at + block].astype(wide)
            ).astype(low_type)
            place[out] += 1


def run_round(folds, after=()):
    arrays, jobs, shapes, counts = [], [], [], []

    def slot(array):
        for i, known in enumerate(arrays):
            if known is array:
                return i
        arrays.append(array)
        return len(arrays) - 1

    listed = []
    for fold in folds:
        fold_jobs, outs = fold.jobs()
        for part, blocks, out in fold_jobs:
            keep, keep_at = part.keep
            got, got_at = part.got
            listed.append((slot(keep), slot(got), blocks, keep_at, got_at, len(shapes) + out))
        shapes += outs
        counts.append(len(outs))
    if not shapes:
        return []
    first_out = len(arrays) + len(after)
    jobs = [job[:5] + (first_out + job[5],) for job in listed]
    outs = pl.pallas_call(
        functools.partial(round_kernel, jobs),
        in_specs=[pl.BlockSpec(memory_space=pltpu.VMEM)] * len(arrays)
        + [pl.BlockSpec(memory_space=pl.ANY)] * len(after),
        out_specs=[pl.BlockSpec(memory_space=pltpu.VMEM)] * len(shapes),
        out_shape=[shape_of(dims, low_type) for dims in shapes],
        compiler_params=pltpu.CompilerParams(vmem_limit_bytes=58 * 2**20),
        name="round",
    )(*arrays, *after)
    sent = []
    for fold, count in zip(folds, counts):
        sent += fold.take(outs[:count])
        outs = outs[count:]
    return sent


def finish_kernel(here_ref, *refs):
    ins, (qkv_ref, proj_ref, up_ref, down_ref, at_ref, ff_ref) = refs[:-6], refs[-6:]
    rows, width = proj_ref.shape[1:]
    for layer in range(LAYERS):
        at, ff = ins[:SLABS], ins[SLABS : 2 * SLABS]
        ins = ins[2 * SLABS :]
        for step in range(SLABS):
            place = jnp.bitwise_xor(here_ref[1], step)
            at_ref[place] = at[step][0]
            ff_ref[place] = ff[step][...]
        for place in range(SLABS):
            cols = slice(place * width, (place + 1) * width)
            if place < 3:
                qkv_ref[layer, :, cols] = at_ref[place].astype(wide)
            else:
                proj_ref[layer] = at_ref[place].astype(wide)
            up_ref[layer, :, cols] = ff_ref[place, 0].astype(wide)
            down_ref[layer, place * rows : (place + 1) * rows] = ff_ref[place, 1].astype(wide)


def finish(here, owned):
    arrays = [part for at, ff in owned for part in (*at, *ff)]
    rows, width = owned[0][0][0].shape[1:]
    outs = [
        shape_of((LAYERS, rows, 3 * width), wide),
        shape_of((LAYERS, rows, width), wide),
        shape_of((LAYERS, rows, SLABS * width), wide),
        shape_of((LAYERS, SLABS * rows, width), wide),
    ]
    return pl.pallas_call(
        finish_kernel,
        grid_spec=pltpu.PrefetchScalarGridSpec(
            num_scalar_prefetch=1,
            grid=(1,),
            in_specs=[full(part.shape) for part in arrays],
            out_specs=[full(out.shape) for out in outs],
            scratch_shapes=[
                pltpu.VMEM((SLABS, rows, width), low_type),
                pltpu.VMEM((SLABS, 2, rows, width), low_type),
            ],
        ),
        out_shape=outs,
        compiler_params=pltpu.CompilerParams(vmem_limit_bytes=58 * 2**20),
        name="finish",
    )(here, *arrays)


def finish_plain(here, owned, places):
    found = [[], [], [], []]
    order = jnp.bitwise_xor(jnp.arange(places, dtype=jnp.int32), here[1])
    for at, ff in owned:
        at = jnp.take(jnp.stack(at), order, axis=0)[:, 0].astype(wide)
        ff = jnp.take(jnp.stack(ff), order, axis=0).transpose(1, 0, 2, 3).astype(wide)
        width = at.shape[-1]
        at = at.reshape(SLABS, -1, width)
        ff = ff.reshape(2, SLABS, -1, width)
        rows = at.shape[1]
        found[0].append(at[:3].transpose(1, 0, 2).reshape(rows, 3 * width))
        found[1].append(at[3])
        found[2].append(ff[0].transpose(1, 0, 2).reshape(rows, SLABS * width))
        found[3].append(ff[1].reshape(SLABS * rows, width))
    return [jnp.stack(each) for each in found]


def place_kernel(here_ref, own_ref, own_far_ref, *refs):
    near, far, out_ref = refs[:4], refs[4:8], refs[8]
    replica = here_ref[1]
    pair = pl.program_id(0) // 2
    odd = pl.program_id(0) % 2
    half = out_ref.shape[3] // 2
    for parity, own, parts in ((0, own_ref, near), (1, own_far_ref, far)):

        @pl.when(jnp.logical_and(pair == 0, odd == parity))
        def _():
            for place in range(SLABS):
                out_ref[place, 0] = own[place]

        @pl.when(jnp.logical_and(pair > 0, odd == parity))
        def _():
            for part, steps, low in zip(parts, ((0, 1), (2, 3), (0, 2), (1, 3)), (0, 0, half, half)):
                for i, step in enumerate(steps):
                    place = jnp.bitwise_xor(replica, step)
                    for k in range(out_ref.shape[2]):
                        out_ref[place, 0, k, low : low + half] = part[i, 0, k]


def place_weights(net, here, own, own_far, near, far):
    places, kinds, rows, width = own.shape
    half = rows // 2
    whole = pl.BlockSpec(own.shape, lambda g, here_ref: (0, 0, 0, 0))
    part = pl.BlockSpec(
        (2, 1, kinds, half, width),
        lambda g, here_ref: (0, jnp.maximum(g // 2 - 1, 0), 0, 0, 0),
    )

    def target(g, here_ref):
        pair = g // 2
        step = (pair % 2) * 4 + (pair // 2) * 2 + g % 2
        return (0, jnp.bitwise_xor(here_ref[0], step), 0, 0, 0)

    return pl.pallas_call(
        place_kernel,
        grid_spec=pltpu.PrefetchScalarGridSpec(
            num_scalar_prefetch=1,
            grid=(net.shards,),
            in_specs=[whole, whole] + [part] * 8,
            out_specs=pl.BlockSpec((places, 1, kinds, rows, width), target),
        ),
        out_shape=shape_of((places, net.shards, kinds, rows, width), low_type),
        compiler_params=pltpu.CompilerParams(vmem_limit_bytes=56 * 2**20),
        name="place_weights",
    )(here, own, own_far, *near, *far)


def gather_steps(net, here, packed):
    own_far = net.swap(packed, "shard", 1)
    mine = lax.dynamic_index_in_dim(packed, here[1], 0, keepdims=True)
    got = net.swap(mine, "shard", 4)
    yield [mine]
    both = jnp.concatenate([mine, got])
    more = net.swap(both, "shard", 2)
    yield [both]
    half = packed.shape[2] // 2
    halves = []
    for cut in (slice(0, half), slice(half, None)):
        halves.append(jnp.concatenate([got[:, :, cut], more[:, :, cut]])[None])
    gots = [net.swap(part, "replica", step) for part, step in zip(halves, (1, 2))]
    yield halves
    firsts = [jnp.concatenate([part, came]) for part, came in zip(halves, gots)]
    seconds = [net.swap(part, "replica", step) for part, step in zip(firsts, (2, 1))]
    firsts_far = [net.swap(part, "shard", 1) for part in firsts]
    yield firsts
    seconds_far = [net.swap(part, "shard", 1) for part in seconds]
    yield seconds
    near = [firsts[0], seconds[0], firsts[1], seconds[1]]
    far = [firsts_far[0], seconds_far[0], firsts_far[1], seconds_far[1]]
    return place_weights(net, here, packed, own_far, near, far)


def gather_whole(net, here, packed):
    mine = lax.dynamic_index_in_dim(packed, here[1], 0, keepdims=False)
    flat = mine.reshape(-1, mine.shape[-1])
    whole = lax.all_gather(flat, ("replica", "shard"), axis=0, tiled=True)
    return whole.reshape((net.replicas, net.shards) + mine.shape)


def plain_slabs(net, whole, tall_kind):
    places, shards, kinds, part, width = whole.shape
    split = whole.reshape(SLABS, places // SLABS, shards, kinds, part, width)
    split = split.transpose(3, 0, 2, 1, 4, 5).reshape(kinds, SLABS, shards, -1, width)
    made = []
    for kind in range(kinds):
        each = split[kind]
        if kind == tall_kind:
            each = each.transpose(1, 0, 2, 3)
        made.append(each.reshape(SLABS, 1, width, width))
    return jnp.stack(made, axis=2)


class Steps:
    def __init__(self, steps):
        self.steps = steps
        self.result = None
        self.over = False

    def go(self, count=1):
        sent = []
        for _ in range(count):
            if not self.over:
                try:
                    sent = next(self.steps)
                except StopIteration as end:
                    self.over = True
                    self.result = end.value
                    sent = []
        return list(sent)

    def end(self):
        while not self.over:
            self.go()
        return self.result


def local(
    net,
    hidden_in,
    condition,
    latent_live,
    out_grad,
    ada_weight,
    qkv_weight,
    proj_weight,
    fc1_weight,
    fc2_weight,
    ada_bias,
    qv_bias,
    proj_bias,
    fc1_bias,
    fc2_bias,
):
    shard = lax.axis_index("shard")
    replica = lax.axis_index("replica")
    here = jnp.stack([shard, replica]).astype(jnp.int32)
    shards, replicas = net.shards, net.replicas
    latents_here, model_width = condition.shape
    rows = proj_weight.shape[1]
    piece_rows = rows * SLABS // replicas
    mod_width = ada_weight.shape[2]

    fused = replicas == SLABS and shards == 2 * SLABS and rows % 16 == 0

    def pack(layer):
        qkv = qkv_weight[layer].astype(low_type)
        up = fc1_weight[layer].astype(low_type)
        down = fc2_weight[layer].astype(low_type)
        columns = lambda w, b: w[:, b * model_width : (b + 1) * model_width]
        attn = [columns(qkv, b) for b in range(3)] + [proj_weight[layer].astype(low_type)]
        kinds = [jnp.stack(attn), jnp.stack([columns(up, b) for b in range(SLABS)]), down]
        return [kind.reshape(replicas, 1, piece_rows, model_width) for kind in kinds]

    packs = [pack(layer) for layer in range(LAYERS)]
    if fused:
        a0 = Steps(gather_steps(net, here, packs[0][0]))
        f0 = Steps(gather_steps(net, here, jnp.concatenate(packs[0][1:], axis=1)))
        later = gather_whole(net, here, jnp.concatenate(packs[1], axis=1))
    else:
        wholes = [
            plain_slabs(net, gather_whole(net, here, jnp.concatenate(kinds, axis=1)), 2)
            for kinds in packs
        ]

    cond_low = jax.nn.silu(condition).astype(low_type)
    bias_rows = jnp.concatenate([qv_bias, proj_bias, fc1_bias, fc2_bias], axis=1).astype(low_type)
    bias_width = bias_rows.shape[1]
    bias_rows = jnp.pad(bias_rows, ((0, 0), (0, model_width - bias_width)))
    both_rel = net.gather_rel(jnp.concatenate([cond_low, bias_rows]), ["shard"])
    cond_rel = both_rel[:, :latents_here]
    found = net.order("shard")
    spots = jnp.array([found.index(step) for step in range(shards)], jnp.int32)
    order = jnp.take(spots, jnp.bitwise_xor(jnp.arange(shards, dtype=jnp.int32), here[0]))
    bias_all = jnp.take(both_rel[:, latents_here:], order, axis=0)
    cond_steps = Steps(net.gather_steps(cond_rel, "replica"))
    group = shards * latents_here
    cond_rows = lax.dynamic_slice_in_dim(
        cond_rel.reshape(group, model_width), shard * rows, rows, axis=1
    )
    ada_low = ada_weight.astype(low_type)
    partial = jnp.stack([nn(cond_rows, ada_low[layer]) for layer in range(LAYERS)], axis=1)
    ada_part = ada_bias.shape[1]
    bias_here = lax.dynamic_update_slice_in_dim(
        jnp.zeros((LAYERS, mod_width), wide),
        ada_bias.astype(low_type).astype(wide),
        shard * ada_part,
        axis=1,
    )
    partial = (partial + bias_here[None]).reshape(shards, latents_here, LAYERS, mod_width)
    modulations = net.scatter_rel(partial)

    widths = (qv_bias.shape[1], proj_bias.shape[1], fc1_bias.shape[1], fc2_bias.shape[1])
    starts = (0, widths[0], widths[0] + widths[1], widths[0] + widths[1] + widths[2])

    def biases_of(layer):
        qv, proj, up, down = [
            bias_all[:, layer, start : start + width].reshape(-1).astype(wide)
            for start, width in zip(starts, widths)
        ]
        qkv_b = jnp.stack([qv[:model_width], jnp.zeros((model_width,), wide), qv[model_width:]])
        up_b = up.reshape(SLABS, 1, model_width)
        return (qkv_b[:, None], proj[None], up_b, down[None])

    def attn_first():
        a0.go(2)
        a0.go(), f0.go()
        a0.go(), f0.go()
        a0.go()
        after = f0.go()
        return (a0.end(), 0), after

    def feed_first():
        both = f0.end()
        return (both, 0), (both, 1), cond_steps.go()

    if fused:
        attn_calls = (attn_first, lambda: ((later, 0), []))
        feed_calls = (feed_first, lambda: ((later, 1), (later, 2), cond_steps.go()))
        slot_calls = (lambda: f0.go(), lambda: [])
    else:
        attn_calls = [lambda w=w: ((w, 0), []) for w in wholes]
        feed_calls = [lambda w=w: ((w, 1), (w, 2), []) for w in wholes]
        slot_calls = [lambda: []] * LAYERS

    live_rows = latent_live.astype(wide)[:, None, None]
    saved_all = []
    current = hidden_in
    weights_all = []
    for layer in range(LAYERS):
        current, saved_state, layer_weights = forward_layer(
            here,
            current,
            modulations[:, layer].reshape(latents_here, 6, model_width),
            attn_calls[layer],
            feed_calls[layer],
            biases_of(layer),
            slot_calls[layer],
        )
        saved_all.append(saved_state)
        weights_all.append(layer_weights)
    result = current * live_rows
    grad_now = out_grad * live_rows

    def send(grads):
        if fused:
            return Fold(net, list(zip(grads[::2], grads[1::2])))
        slabs = [grads[0].reshape(SLABS, shards, rows, model_width)]
        if len(grads) > 1:
            down = grads[1].reshape(shards, SLABS, rows, model_width)
            slabs.append(down.transpose(1, 0, 2, 3))
        pairs = [[half[0] for half in order_grads(net, here, each)] for each in slabs]
        return Steps(reduce_steps(net, here, pairs))

    sends = {}
    bias_steps = [None]

    def bias_row(layer, sums, up_sums, down_sums):
        grads = (
            jnp.concatenate([sums[0], sums[2]]),
            sums[3],
            up_sums.reshape(-1),
            down_sums[0],
        )
        bias_sums[layer] = jnp.concatenate([grad.reshape(shards, -1) for grad in grads], axis=1)
        if layer == 0:
            bias_steps[0] = Steps(net.total_steps(jnp.stack(bias_sums)))

    def middle_slot(layer):
        def slot(ff_grads):
            fold = sends["ff", layer] = send(ff_grads)
            if not fused:
                return []
            return fold.sent + (run_round([sends["ff", 1], sends["at", 1]]) if layer == 0 else [])

        return slot

    def late_slot(layer):
        def slot(sums, up_sums, down_sums):
            bias_row(layer, sums, up_sums, down_sums)
            if not fused:
                return []
            if layer == 1:
                return run_round([sends["ff", 1]])
            sent = bias_steps[0].go()
            return sent + run_round([sends["ff", 1], sends["at", 1], sends["ff", 0]])

        return slot

    ada_wide = ada_low.astype(wide)
    grad_cond = jnp.zeros((group, rows), wide)
    ada_grads = [None] * LAYERS
    modul_grads = [None] * LAYERS
    bias_sums = [None] * LAYERS
    for layer in reversed(range(LAYERS)):
        before = sends["at", 1].sent if layer == 0 and fused else []
        grad_now, grad_modul, at_grads = backward_layer(
            here,
            fused,
            grad_now,
            weights_all[layer],
            saved_all[layer],
            before,
            middle_slot(layer),
            late_slot(layer),
        )
        sends["at", layer] = send(at_grads)
        modul_grads[layer] = grad_modul
    modul_steps = Steps(net.gather_steps(jnp.concatenate(modul_grads), "shard"))
    bias_steps = bias_steps[0]
    ring = [sends["ff", 1], sends["at", 1], sends["ff", 0], sends["at", 0]]
    every_steps = None
    for turn in range(8):
        after = modul_steps.go() + bias_steps.go()
        if modul_steps.over and every_steps is None:
            modul_low = modul_steps.result.astype(low_type)
            every_steps = Steps(net.gather_steps(modul_low, "replica"))
        if every_steps is not None:
            after += every_steps.go()
        if fused:
            run_round(ring, after)
    modul = modul_steps.end()
    modul_low = every_steps.end()
    cond_every = lax.dynamic_slice_in_dim(
        cond_steps.end().reshape(replicas * group, model_width), shard * rows, rows, axis=1
    )
    per_layer = lambda w, layer: w[..., layer * latents_here : (layer + 1) * latents_here, :]
    for layer in range(LAYERS):
        mine = per_layer(modul, layer).reshape(group, mod_width)
        grad_cond = grad_cond + exact_trail(mine, ada_wide[layer])
        every = per_layer(modul_low, layer).reshape(replicas * group, mod_width)
        ada_grads[layer] = tn(cond_every, every)
    own_mod = lax.dynamic_slice_in_dim(modul_low, shard * ada_part, ada_part, axis=3).astype(wide)
    own_mod = own_mod.reshape(replicas * shards, LAYERS, latents_here, ada_part)
    ada_bias_out = jnp.sum(own_mod, axis=(0, 2))
    bias_total = bias_steps.end()
    bias_mine = lax.dynamic_index_in_dim(bias_total, shard, 1, keepdims=False)
    bias_out = [bias_mine[:, start : start + width] for start, width in zip(starts, widths)]

    if fused:
        owned = [(sends["at", layer].every, sends["ff", layer].every) for layer in range(LAYERS)]
        weight_outs = finish(here, owned)
    else:
        owned = [
            (sends["at", layer].end(), sends["ff", layer].end()) for layer in range(LAYERS)
        ]
        weight_outs = finish_plain(here, owned, replicas)
    parts = grad_cond.reshape(shards, latents_here, rows)
    back = [parts[0]]
    back += [net.swap(parts[i], "shard", found[i]) for i in range(1, shards)]
    back = jnp.take(jnp.stack(back), order, axis=0)
    cond_back = back.transpose(1, 0, 2).reshape(latents_here, model_width)
    grad_condition = jax.vjp(jax.nn.silu, condition)[1](cond_back)[0]
    return (
        result,
        grad_now,
        grad_condition,
        jnp.stack(ada_grads),
        *weight_outs,
        ada_bias_out,
        *bias_out,
    )


def solution(mesh):
    tokens = P(("replica", "shard"), None, None)
    weight = P(None, "shard", None)
    bias = P(None, "shard")
    rows = P(("replica", "shard"), None)
    return jax.shard_map(
        functools.partial(local, Net(mesh)),
        mesh=mesh,
        in_specs=(tokens, rows, P(("replica", "shard")), tokens) + (weight,) * 5 + (bias,) * 5,
        out_specs=(tokens, tokens, rows) + (weight,) * 5 + (bias,) * 5,
        check_vma=False,
    )
```

```python
import functools

import jax
import jax.numpy as jnp
from jax import lax
from jax.experimental import pallas as pl
from jax.experimental.pallas import tpu as pltpu
from jax.sharding import PartitionSpec as P

HEADS = 12
HEAD_DIM = 64
LAYERS = 2
SLABS = 4

norm_eps = 1e-06
highest = lax.Precision.HIGHEST
low_type = jnp.bfloat16
wide = jnp.float32


def nn(left, right):
    return lax.dot_general(left, right, (((1,), (0,)), ((), ())), preferred_element_type=wide)


def nt(left, right):
    return lax.dot_general(left, right, (((1,), (1,)), ((), ())), preferred_element_type=wide)


def tn(left, right):
    return lax.dot_general(left, right, (((0,), (0,)), ((), ())), preferred_element_type=wide)


def exact_lead(left_side, right_side):
    return lax.dot_general(
        left_side,
        right_side,
        (((0,), (0,)), ((), ())),
        precision=highest,
        preferred_element_type=wide,
    )


def exact_trail(left_side, right_side):
    return lax.dot_general(
        left_side,
        right_side,
        (((1,), (1,)), ((), ())),
        precision=highest,
        preferred_element_type=wide,
    )


def normalise(rows):
    centred = rows - jnp.mean(rows, axis=-1, keepdims=True)
    spread = jnp.mean(centred * centred, axis=-1, keepdims=True)
    inverse = lax.rsqrt(spread + norm_eps)
    return centred * inverse, inverse


def norm_back(grad, rows, stretch):
    normed, inverse = normalise(rows)
    inner = grad * (1.0 + stretch)
    first = jnp.mean(inner, axis=-1, keepdims=True)
    second = jnp.mean(inner * normed, axis=-1, keepdims=True)
    back = (inner - first - normed * second) * inverse
    return (
        back,
        jnp.sum(grad, axis=0, keepdims=True),
        jnp.sum(grad * normed, axis=0, keepdims=True),
    )


def slab(ref):
    return ref[0].reshape(ref.shape[3], ref.shape[3])


def tall(ref):
    if ref.shape[0] == 1:
        return slab(ref)
    return jnp.concatenate(
        [ref[r, s] for s in range(ref.shape[1]) for r in range(ref.shape[0])], axis=0
    )


def qkv_kernel(x_ref, mod_ref, w_ref, b_ref, u_ref, qkv_ref):
    latents, seq, _ = x_ref.shape

    @pl.when(pl.program_id(0) == 0)
    def _():
        for i in range(latents):
            normed, _ = normalise(x_ref[i])
            u_ref[i * seq : (i + 1) * seq] = (
                normed * (1.0 + mod_ref[i, 1:2]) + mod_ref[i, 0:1]
            ).astype(low_type)

    for i in range(latents):
        part = slice(i * seq, (i + 1) * seq)
        qkv_ref[0, part] = (nn(u_ref[part], slab(w_ref)) + b_ref[0]).astype(low_type)


def mix_kernel(qkv_ref, x_ref, mod_ref, w_ref, b_ref, o_ref, a_ref, x1_ref, u2_ref):
    seq, width = o_ref.shape
    pair = 2 * HEAD_DIM
    lane = lax.broadcasted_iota(jnp.int32, (seq, pair), 1)
    left = lane < HEAD_DIM
    for at in range(0, width, pair):
        query = qkv_ref[0, :, at : at + pair]
        key = qkv_ref[1, :, at : at + pair]
        value = qkv_ref[2, :, at : at + pair]
        mixed = []
        for side in (left, jnp.logical_not(left)):
            raw = nt(jnp.where(side, query, jnp.zeros_like(query)), key) * HEAD_DIM ** (-0.5)
            top = jnp.exp(raw - jnp.max(raw, axis=-1, keepdims=True))
            probs = top * (1.0 / jnp.sum(top, axis=-1, keepdims=True))
            mixed.append(nn(probs.astype(low_type), value))
        o_ref[:, at : at + pair] = jnp.where(left, mixed[0], mixed[1]).astype(low_type)
    branch = nn(o_ref[...], slab(w_ref)) + b_ref[...]
    a_ref[...] = branch
    middle = x_ref[0] + mod_ref[0, 2:3] * branch
    x1_ref[...] = middle
    normed, _ = normalise(middle)
    u2_ref[...] = (normed * (1.0 + mod_ref[0, 4:5]) + mod_ref[0, 3:4]).astype(low_type)


GELU_SCALE = 0.7978845608028654
GELU_CUBE = 0.044715


def feed_kernel(
    u2_ref, x1_ref, mod_ref, up_ref, upb_ref, down_ref, downb_ref, g_ref, slope_ref, m_ref, x_ref
):
    latents = mod_ref.shape[0]
    seq = u2_ref.shape[0] // latents
    step = pl.program_id(0)
    down = tall(down_ref)
    for i in range(latents):
        part = slice(i * seq, (i + 1) * seq)
        pre = nn(u2_ref[part], slab(up_ref)) + upb_ref[0]
        square = pre * pre
        bent = jnp.tanh(GELU_SCALE * (pre + GELU_CUBE * (square * pre)))
        half = 0.5 * (1.0 + bent)
        act = (pre * half).astype(low_type)
        g_ref[0, part] = act
        slope_ref[0, part] = (
            half
            + (0.5 * GELU_SCALE)
            * pre
            * (1.0 - bent * bent)
            * (1.0 + (3.0 * GELU_CUBE) * square)
        ).astype(low_type)
        part_sum = nn(act, down)

        @pl.when(step == 0)
        def _():
            m_ref[part] = part_sum + downb_ref[...]

        @pl.when(step > 0)
        def _():
            m_ref[part] = m_ref[part] + part_sum

        @pl.when(step == pl.num_programs(0) - 1)
        def _():
            x_ref[part] = x1_ref[part] + mod_ref[i, 5:6] * m_ref[part]


def store_slab(here_ref, product, kept_ref, sent_ref, hold_ref):
    hold_ref[...] = product.astype(low_type).reshape(hold_ref.shape)
    for near in range(kept_ref.shape[0]):
        owner = jnp.bitwise_xor(here_ref[0], 2 * near)
        kept_ref[near, 0] = hold_ref[owner]
        sent_ref[near, 0] = hold_ref[jnp.bitwise_xor(owner, 1)]


def feed_back_kernel(
    fused, here_ref, dy_ref, m_ref, mod_ref, u2_ref, g_ref, slope_ref, up_ref, down_ref,
    *refs,
):
    if fused:
        up_grads, down_grads, refs = refs[:2], refs[2:4], refs[4:]
    else:
        up_grad, down_grad, refs = refs[0], refs[1], refs[2:]
    du_ref, dgate_ref, downb_ref, upb_ref, dm_ref, df_ref, hold_ref = refs
    latents = mod_ref.shape[0]
    seq = u2_ref.shape[0] // latents
    step = pl.program_id(0)

    @pl.when(step == 0)
    def _():
        total = jnp.zeros(downb_ref.shape, wide)
        for i in range(latents):
            part = slice(i * seq, (i + 1) * seq)
            grad = dy_ref[part]
            dgate_ref[i] = jnp.sum(grad * m_ref[part], axis=0, keepdims=True)
            lower = (grad * mod_ref[i, 5:6]).astype(low_type)
            dm_ref[part] = lower
            total += jnp.sum(lower.astype(wide), axis=0, keepdims=True)
        downb_ref[...] = total

    sums = jnp.zeros(upb_ref.shape[1:], wide)
    down = tall(down_ref)
    for i in range(latents):
        part = slice(i * seq, (i + 1) * seq)
        lower = (nt(dm_ref[part], down) * slope_ref[0, part].astype(wide)).astype(low_type)
        df_ref[part] = lower
        sums += jnp.sum(lower.astype(wide), axis=0, keepdims=True)
        back = nt(lower, slab(up_ref))

        @pl.when(step == 0)
        def _():
            du_ref[part] = back

        @pl.when(step > 0)
        def _():
            du_ref[part] = du_ref[part] + back

    upb_ref[0] = sums
    down_part = tn(g_ref[0], dm_ref[...])
    up_part = tn(u2_ref[...], df_ref[...])
    if not fused:
        down_grad[0] = down_part.astype(low_type)
        up_grad[0] = up_part.astype(low_type)
        return
    store_slab(here_ref, up_part, up_grads[0], up_grads[1], hold_ref)
    hold_ref[...] = down_part.astype(low_type).reshape(hold_ref.shape)
    places = down_grads[0].shape[1]
    low = here_ref[0] % 2
    for place in range(places):
        piece = jnp.bitwise_xor(here_ref[1], place)
        down_grads[0][0, place] = hold_ref[low * places + piece]
        down_grads[1][0, place] = hold_ref[(1 - low) * places + piece]


def mix_back_kernel(
    du_ref, x1_ref, dy_ref, a_ref, qkv_ref, mod_ref, w_ref,
    dx1_ref, dall_ref, dmod_ref, sums_ref, do_ref,
):
    seq, width = x1_ref.shape
    pair = 2 * HEAD_DIM
    back, dshift, dscale = norm_back(du_ref[...], x1_ref[...], mod_ref[0, 4:5])
    dx1 = back + dy_ref[...]
    dx1_ref[...] = dx1
    dmod_ref[0, 0:1] = dshift
    dmod_ref[0, 1:2] = dscale
    dmod_ref[0, 2:3] = jnp.sum(dx1 * a_ref[...], axis=0, keepdims=True)
    da = (dx1 * mod_ref[0, 2:3]).astype(low_type)
    dall_ref[3] = da
    do_ref[...] = nt(da, slab(w_ref)).astype(low_type)
    lane = lax.broadcasted_iota(jnp.int32, (seq, pair), 1)
    left = lane < HEAD_DIM
    for at in range(0, width, pair):
        cols = slice(at, at + pair)
        query = qkv_ref[0, :, cols]
        key = qkv_ref[1, :, cols]
        value = qkv_ref[2, :, cols]
        grad = do_ref[:, cols]
        found = []
        for side in (left, jnp.logical_not(left)):
            none = jnp.zeros_like(query)
            raw = nt(key, jnp.where(side, query, none)) * HEAD_DIM ** (-0.5)
            top = jnp.exp(raw - jnp.max(raw, axis=0, keepdims=True))
            probs = top * (1.0 / jnp.sum(top, axis=0, keepdims=True))
            dvalue = nn(probs.astype(low_type), grad)
            dprobs = nt(value, jnp.where(side, grad, none))
            dots = jnp.sum(dprobs * probs, axis=0, keepdims=True)
            draw = (probs * (dprobs - dots) * HEAD_DIM ** (-0.5)).astype(low_type)
            found.append((tn(draw, key), nn(draw, query), dvalue))
        for which in range(3):
            dall_ref[which, :, cols] = jnp.where(
                left, found[0][which], found[1][which]
            ).astype(low_type)

    @pl.when(pl.program_id(0) == 0)
    def _():
        sums_ref[...] = jnp.zeros_like(sums_ref)

    for which in range(4):
        sums_ref[which : which + 1] += jnp.sum(
            dall_ref[which].astype(wide), axis=0, keepdims=True
        )


def qkv_back_kernel(
    fused, here_ref, u1_ref, o_ref, dall_ref, w_ref, x_ref, dx1_ref, mod_ref, *refs
):
    grads = refs[:2] if fused else refs[:1]
    dx_ref, dmod_ref, acc_ref, hold_ref = refs[len(grads) :]

    def store(product):
        if fused:
            store_slab(here_ref, product, grads[0], grads[1], hold_ref)
        else:
            grads[0][0] = product.astype(low_type)

    latents, seq, _ = x_ref.shape
    step = pl.program_id(0)

    @pl.when(step < 3)
    def _():
        store(tn(u1_ref[...], dall_ref[0]))
        for i in range(latents):
            part = slice(i * seq, (i + 1) * seq)
            back = nt(dall_ref[0, part], slab(w_ref))

            @pl.when(step == 0)
            def _():
                acc_ref[part] = back

            @pl.when(step > 0)
            def _():
                acc_ref[part] = acc_ref[part] + back

    @pl.when(step == 3)
    def _():
        store(tn(o_ref[...], dall_ref[0]))
        for i in range(latents):
            part = slice(i * seq, (i + 1) * seq)
            back, dshift, dscale = norm_back(acc_ref[part], x_ref[i], mod_ref[i, 1:2])
            dx_ref[i] = back + dx1_ref[part]
            dmod_ref[i, 0:1] = dshift
            dmod_ref[i, 1:2] = dscale


def shape_of(dims, kind):
    return jax.ShapeDtypeStruct(tuple(dims), kind)


def full(dims):
    return pl.BlockSpec(tuple(dims), lambda step, here_ref: (0,) * len(dims))


def along(dims, where):
    return pl.BlockSpec(
        tuple(dims),
        lambda step, here_ref: tuple(step if i == where else 0 for i in range(len(dims))),
    )


def slab_spec(weight, fixed=None):
    array, kind = weight
    _, shards, _, rows, width = array.shape
    return pl.BlockSpec(
        (1, shards, None, rows, width),
        lambda step, here_ref: (step if fixed is None else fixed, 0, kind, 0, 0),
    )


def tall_spec(weight):
    array, kind = weight
    slabs, shards, _, rows, width = array.shape
    if shards == 1:
        return slab_spec(weight)
    return pl.BlockSpec(
        (slabs, shards // slabs, None, rows, width), lambda step, here_ref: (0, step, kind, 0, 0)
    )


def call(
    kernel, here, grid, in_specs, out_specs, out_shape, scratch, flops, moved, after=(), fused=None
):
    count = len(in_specs)

    def body(here_ref, *refs):
        lead = () if fused is None else (fused, here_ref)
        kernel(*lead, *refs[:count], *refs[count + len(after) :])

    run = pl.pallas_call(
        body,
        grid_spec=pltpu.PrefetchScalarGridSpec(
            num_scalar_prefetch=1,
            grid=(grid,),
            in_specs=list(in_specs) + [pl.BlockSpec(memory_space=pl.ANY)] * len(after),
            out_specs=out_specs,
            scratch_shapes=scratch,
        ),
        out_shape=out_shape,
        compiler_params=pltpu.CompilerParams(vmem_limit_bytes=58 * 2**20),
        cost_estimate=pl.CostEstimate(flops=flops, bytes_accessed=moved, transcendentals=0),
        name=kernel.__name__,
    )
    return lambda *arrays: run(here, *arrays, *after)


def forward_layer(here, hidden, mod, attn, feed, biases, slots):
    qkv_b, proj_b, up_b, down_b = biases
    attn_w, after = attn()
    latents, seq, width = hidden.shape
    rows = latents * seq
    unit = 2 * rows * width * width
    size = rows * width
    u1, qkv = call(
        qkv_kernel,
        here,
        3,
        [
            full(hidden.shape),
            full(mod.shape),
            slab_spec(attn_w),
            along((1, 1, width), 0),
        ],
        [full((rows, width)), along((1, rows, width), 0)],
        [shape_of((rows, width), low_type), shape_of((3, rows, width), low_type)],
        [],
        3 * unit,
        18 * size,
        after,
    )(hidden, mod, attn_w[0], qkv_b)
    token = along((seq, width), 0)
    mixed, branch, middle, u2 = call(
        mix_kernel,
        here,
        latents,
        [
            along((3, seq, width), 1),
            along((1, seq, width), 0),
            along((1, 6, width), 0),
            slab_spec(attn_w, 3),
            full((1, width)),
        ],
        [token, token, token, token],
        [
            shape_of((rows, width), low_type),
            shape_of((rows, width), wide),
            shape_of((rows, width), wide),
            shape_of((rows, width), low_type),
        ],
        [],
        5 * unit,
        24 * size,
        slots(),
    )(qkv, hidden, mod, attn_w[0], proj_b)
    up_w, down_w, after = feed()
    act, slope, branch_two, result = call(
        feed_kernel,
        here,
        SLABS,
        [
            full((rows, width)),
            full((rows, width)),
            full(mod.shape),
            slab_spec(up_w),
            along((1, 1, width), 0),
            tall_spec(down_w),
            full((1, width)),
        ],
        [
            along((1, rows, width), 0),
            along((1, rows, width), 0),
            full((rows, width)),
            full((rows, width)),
        ],
        [
            shape_of((SLABS, rows, width), low_type),
            shape_of((SLABS, rows, width), low_type),
            shape_of((rows, width), wide),
            shape_of((rows, width), wide),
        ],
        [],
        12 * unit,
        40 * size,
        after,
    )(u2, middle, mod, up_w[0], up_b, down_w[0], down_b)
    saved = (hidden, mod, u1, qkv, mixed, branch, middle, u2, act, slope, branch_two)
    return result.reshape(hidden.shape), saved, (attn_w, up_w, down_w)


def backward_layer(here, fused, grad_out, weights, saved, before, middle_slot, late_slot):
    attn_w, up_w, down_w = weights
    hidden, mod, u1, qkv, mixed, branch, middle, u2, act, slope, branch_two = saved
    latents, seq, width = hidden.shape
    rows = latents * seq
    unit = 2 * rows * width * width
    size = rows * width
    grad_out = grad_out.reshape(rows, width)
    block = along((1, rows, width), 0)
    flat = full((rows, width))
    square = along((1, width, width), 0)
    _, shards, _, own, _ = attn_w[0].shape
    near = shards // 2
    by_place = pl.BlockSpec(
        (near, 1, own, width),
        lambda step, here_ref: (0, jnp.bitwise_xor(here_ref[1], step), 0, 0),
    )
    by_near = pl.BlockSpec(
        (1, SLABS, own, width),
        lambda step, here_ref: (jnp.bitwise_xor(here_ref[0] // 2, step), 0, 0, 0),
    )
    half = shape_of((near, SLABS, own, width), low_type)
    natural = shape_of((SLABS, width, width), low_type)
    hold = pltpu.VMEM((shards, own, width), low_type)
    *ff_grads, du2, dgate_two, down_sums, up_sums = call(
        feed_back_kernel,
        here,
        SLABS,
        [flat, flat, full(mod.shape), flat, block, block, slab_spec(up_w), tall_spec(down_w)],
        ([by_place, by_place, by_near, by_near] if fused else [square, square])
        + [flat, full((latents, 1, width)), full((1, width)), along((1, 1, width), 0)],
        ([half] * 4 if fused else [natural] * 2)
        + [
            shape_of((rows, width), wide),
            shape_of((latents, 1, width), wide),
            shape_of((1, width), wide),
            shape_of((SLABS, 1, width), wide),
        ],
        [pltpu.VMEM((rows, width), low_type), pltpu.VMEM((rows, width), low_type), hold],
        16 * unit,
        50 * size,
        before,
        fused,
    )(grad_out, branch_two, mod, u2, act, slope, up_w[0], down_w[0])
    token = along((seq, width), 0)
    dx1, dall, dmod_mid, sums = call(
        mix_back_kernel,
        here,
        latents,
        [
            token,
            token,
            token,
            token,
            along((3, seq, width), 1),
            along((1, 6, width), 0),
            slab_spec(attn_w, 3),
        ],
        [
            token,
            along((4, seq, width), 1),
            along((1, 3, width), 0),
            full((4, width)),
        ],
        [
            shape_of((rows, width), wide),
            shape_of((4, rows, width), low_type),
            shape_of((latents, 3, width), wide),
            shape_of((4, width), wide),
        ],
        [pltpu.VMEM((seq, width), low_type)],
        10 * unit,
        40 * size,
        middle_slot(ff_grads),
    )(du2, middle, grad_out, branch, qkv, mod, attn_w[0])
    *at_grads, dx, dmod_low = call(
        qkv_back_kernel,
        here,
        4,
        [flat, flat, block, slab_spec(attn_w), full(hidden.shape), flat, full(mod.shape)],
        ([by_place, by_place] if fused else [square])
        + [full(hidden.shape), full((latents, 2, width))],
        ([half] * 2 if fused else [natural])
        + [shape_of(hidden.shape, wide), shape_of((latents, 2, width), wide)],
        [pltpu.VMEM((rows, width), wide), hold],
        7 * unit,
        36 * size,
        late_slot(sums, up_sums, down_sums),
        fused,
    )(u1, mixed, dall, attn_w[0], hidden, dx1, mod)
    dmod = jnp.concatenate(
        [dmod_low, dmod_mid[:, 2:3], dmod_mid[:, 0:2], dgate_two], axis=1
    ).reshape(latents, 6 * width)
    return dx, dmod, at_grads


class Net:
    def __init__(self, mesh):
        self.replicas = mesh.shape["replica"]
        self.shards = mesh.shape["shard"]

    def swap(self, values, axis, step):
        count = self.replicas if axis == "replica" else self.shards
        return lax.ppermute(values, axis, [(i, i ^ step) for i in range(count)])

    def bits(self, axis):
        count = self.replicas if axis == "replica" else self.shards
        found = []
        step = 1
        while step < count:
            found.append(step)
            step *= 2
        return found

    def gather_rel(self, values, axes):
        stack = values[None]
        for axis in axes:
            for step in self.bits(axis)[::-1]:
                stack = jnp.concatenate([stack, self.swap(stack, axis, step)])
        return stack

    def order(self, axis):
        found = [0]
        for step in self.bits(axis)[::-1]:
            found = found + [place ^ step for place in found]
        return found

    def scatter_rel(self, stack):
        for step in self.bits("shard"):
            half = stack.shape[0] // 2
            stack = stack[:half] + self.swap(stack[half:], "shard", step)
        return stack[0]


def order_kernel(places, pieces_per_slab, here_ref, near_ref, keep_ref, send_ref):
    shard_low = here_ref[0] % 2
    replica = here_ref[1]
    for place in range(places):
        piece = jnp.bitwise_xor(replica, place)
        slab = piece // pieces_per_slab
        part = piece % pieces_per_slab
        keep_ref[0, place] = near_ref[slab, shard_low, part].astype(keep_ref.dtype)
        send_ref[0, place] = near_ref[slab, 1 - shard_low, part].astype(send_ref.dtype)


def order_grads(net, here, grads):
    slabs, shards, rows, width = grads.shape
    per_slab = net.replicas // SLABS if net.replicas > SLABS else 1
    places = net.replicas
    if net.replicas < SLABS:
        raise ValueError("replicas")
    piece_rows = rows * SLABS // places
    groups = slabs // SLABS
    view = grads.reshape(groups, SLABS, shards, per_slab, piece_rows, width)
    out = jax.ShapeDtypeStruct((groups, shards // 2, places, piece_rows, width), low_type)
    spec = pl.BlockSpec(
        (None, 1, places, piece_rows, width), lambda g, j, here_ref: (g, j, 0, 0, 0)
    )
    return pl.pallas_call(
        functools.partial(order_kernel, places, per_slab),
        grid_spec=pltpu.PrefetchScalarGridSpec(
            num_scalar_prefetch=1,
            grid=(groups, shards // 2),
            in_specs=[
                pl.BlockSpec(
                    (None, SLABS, 2, per_slab, piece_rows, width),
                    lambda g, j, here_ref: (
                        g,
                        0,
                        jnp.bitwise_xor(here_ref[0] // 2, j),
                        0,
                        0,
                        0,
                    ),
                )
            ],
            out_specs=[spec, spec],
        ),
        out_shape=[out, out],
        name="order_grads",
    )(here, view)


def add_low(left, right):
    return (left.astype(wide) + right.astype(wide)).astype(low_type)


def halve(stack, dim, where):
    size = stack.shape[dim]
    shape = stack.shape[:dim] + (size // (2 * where), 2, where) + stack.shape[dim + 1 :]
    view = stack.reshape(shape)
    rest = stack.shape[:dim] + (size // 2,) + stack.shape[dim + 1 :]
    return (
        lax.index_in_dim(view, 0, dim + 1, keepdims=False).reshape(rest),
        lax.index_in_dim(view, 1, dim + 1, keepdims=False).reshape(rest),
    )


def reduce_steps(net, here, pairs):
    gots = [net.swap(give, "shard", 1) for _, give in pairs]
    yield [give for _, give in pairs]
    near, places, rows, width = pairs[0][0].shape
    single = len(pairs) == 1
    if single:
        cuts = [slice(0, near // 2), slice(near // 2, near)]
        parts = [add_low(pairs[0][0][cut], gots[0][cut]) for cut in cuts]
    else:
        parts = [add_low(keep, got) for (keep, _), got in zip(pairs, gots)]
    lefts = [list(range(places))] * 2
    for steps in zip(net.bits("replica"), net.bits("replica")[::-1]):
        splits = []
        for i, step in enumerate(steps):
            where = sum(1 for q in lefts[i] if q < step)
            splits.append(halve(parts[i], 1, where))
            lefts[i] = [q for q in lefts[i] if not q & step]
        gots = [net.swap(give, "replica", step) for (_, give), step in zip(splits, steps)]
        yield [give for _, give in splits]
        parts = [add_low(keep, got) for (keep, _), got in zip(splits, gots)]
    parts = [part[:, 0] for part in parts]
    steps = net.bits("shard")[1:]
    for step in steps[:-1] if single else steps:
        splits = [halve(part, 0, 1) for part in parts]
        gots = [net.swap(give, "shard", step) for _, give in splits]
        yield [give for _, give in splits]
        parts = [add_low(keep, got) for (keep, _), got in zip(splits, gots)]
    if single:
        got = net.swap(parts[1], "shard", steps[-1])
        yield [parts[1]]
        mine = add_low(parts[0], got)
    else:
        mine = jnp.concatenate(parts)
    every = [mine] + [net.swap(mine, "replica", step) for step in range(1, places)]
    yield [mine]
    return every


class Part:
    def __init__(self, keep, labels, route):
        self.keep = keep
        self.got = None
        self.labels = labels
        self.route = route


class Fold:
    def __init__(self, net, pairs, lazy):
        self.net = net
        near, places, rows, width = pairs[0][0].shape
        ahead = [("replica", step) for step in net.bits("replica")]
        behind = ahead[::-1]
        shard_route = [("shard", step) for step in net.bits("shard")[1:]]
        flat = (near * places, rows, width)
        keeps = [keep.reshape(flat) for keep, _ in pairs]
        gives = [give.reshape(flat) for _, give in pairs]
        self.lazy = lazy
        self.gives = gives
        self.sent = [] if lazy else gives
        self.gots = [None if lazy else net.swap(give, "shard", 1) for give in gives]
        labels = [(2 * t, q) for t in range(near) for q in range(places)]
        self.single = len(pairs) == 1
        if self.single:
            half = len(labels) // 2
            self.parts = [
                Part((keeps[0], 0), labels[:half], ahead + shard_route[:-1]),
                Part((keeps[0], half), labels[half:], behind + shard_route[:-1]),
            ]
            self.last = shard_route[-1]
            starts = (0, half)
        else:
            self.parts = [
                Part((keeps[0], 0), labels, ahead + shard_route),
                Part((keeps[1], 0), labels, behind + shard_route),
            ]
            starts = (0, 0)
        self.starts = starts
        self.every = None
        self.merge = False
        self.arm()

    def arm(self):
        gots = self.gots * 2 if self.single else self.gots
        for part, got, start in zip(self.parts, gots, self.starts):
            part.got = (got, start)

    def jobs(self):
        if self.every is not None:
            return [], []
        first = self.parts[0]
        rows, width = first.keep[0].shape[1:]
        if self.lazy:
            shapes = [give.shape for give in self.gives]
            return [(give, None, i) for i, give in enumerate(self.gives)], shapes
        if self.merge or not first.route:
            if self.single and not self.merge:
                a, b = self.parts
                return [(a, [0], 0), (b, [0], 1)], [(1, rows, width)] * 2
            parts = self.parts[:1] if self.single else self.parts
            jobs = [(part, [0], 0) for part in parts]
            return jobs, [(len(parts), rows, width)]
        jobs, outs = [], []
        for part in self.parts:
            axis, step = part.route[0]
            which = 0 if axis == "shard" else 1
            stay = [i for i, label in enumerate(part.labels) if not label[which] & step]
            leave = [i for i, label in enumerate(part.labels) if label[which] & step]
            for blocks in (stay, leave):
                jobs.append((part, blocks, len(outs)))
                outs.append((len(blocks), rows, width))
        return jobs, outs

    def take(self, outs):
        if self.every is not None:
            return []
        net = self.net
        if self.lazy:
            self.lazy = False
            self.gots = [net.swap(give, "shard", 1) for give in outs]
            self.arm()
            return list(outs)
        if self.merge or not self.parts[0].route:
            if self.single and not self.merge:
                self.merge = True
                axis, step = self.last
                self.parts[0].keep = (outs[0], 0)
                self.parts[0].got = (net.swap(outs[1], axis, step), 0)
                return [outs[1]]
            mine = outs[0]
            self.every = [mine]
            self.every += [net.swap(mine, "replica", step) for step in range(1, net.replicas)]
            return [mine]
        sent = []
        for part, (keep, give) in zip(self.parts, zip(outs[::2], outs[1::2])):
            (axis, step), part.route = part.route[0], part.route[1:]
            which = 0 if axis == "shard" else 1
            part.labels = [label for label in part.labels if not label[which] & step]
            part.keep = (keep, 0)
            part.got = (net.swap(give, axis, step), 0)
            sent.append(give)
        return sent


class Line:
    def __init__(self, net, value, axes, sums=False, lower_at=None):
        self.net = net
        self.value = value
        self.sums = sums
        self.lower_at = lower_at
        self.route = [(axis, step) for axis in axes for step in net.bits(axis)[::-1]]
        self.count = 0
        self.full = None
        self.got = None
        self.over = False
        self.sent = self.send()

    def send(self):
        if not self.route:
            self.over = True
            return []
        axis, step = self.route.pop(0)
        self.got = self.net.swap(self.value, axis, step)
        return [self.value]

    def outs(self):
        if self.over:
            return []
        dims = self.value.shape
        if not self.sums:
            dims = (2 * dims[0],) + dims[1:]
        outs = [shape_of(dims, self.value.dtype)]
        if self.count + 1 == self.lower_at:
            outs.append(shape_of(dims, low_type))
        return outs

    def take(self, outs):
        if self.over:
            return []
        self.count += 1
        self.value = outs[0]
        if self.count == self.lower_at:
            self.full, self.value = outs
        return self.send()

    def end(self):
        while not self.over:
            if self.sums:
                both = self.value + self.got
            else:
                both = jnp.concatenate([self.value, self.got])
            self.take([both.astype(out.dtype) for out in self.outs()])
        return self.value


def line_kernel(sums, value_ref, got_ref, *out_refs):
    count = value_ref.shape[0]
    for out_ref in out_refs:
        if sums:
            out_ref[...] = value_ref[...] + got_ref[...]
        else:
            out_ref[:count] = value_ref[...].astype(out_ref.dtype)
            out_ref[count:] = got_ref[...].astype(out_ref.dtype)


def round_kernel(jobs, line_jobs, *refs):
    for sums, value, got, outs in line_jobs:
        line_kernel(sums, refs[value], refs[got], *[refs[out] for out in outs])
    place = [0] * 64
    for keep, got, blocks, keep_at, got_at, out in jobs:
        if blocks is None:
            refs[out][...] = refs[keep][...]
            continue
        for block in blocks:
            refs[out][place[out]] = (
                refs[keep][keep_at + block].astype(wide) + refs[got][got_at + block].astype(wide)
            ).astype(low_type)
            place[out] += 1


def run_round(folds, lines=(), after=()):
    arrays, jobs, shapes, counts = [], [], [], []

    def slot(array):
        for i, known in enumerate(arrays):
            if known is array:
                return i
        arrays.append(array)
        return len(arrays) - 1

    listed = []
    for fold in folds:
        fold_jobs, outs = fold.jobs()
        for part, blocks, out in fold_jobs:
            if blocks is None:
                place = slot(part)
                listed.append((place, place, None, 0, 0, len(shapes) + out))
                continue
            keep, keep_at = part.keep
            got, got_at = part.got
            listed.append((slot(keep), slot(got), blocks, keep_at, got_at, len(shapes) + out))
        shapes += outs
        counts.append(len(outs))
    shapes = [shape_of(dims, low_type) for dims in shapes]
    line_listed = []
    for line in lines:
        outs = line.outs()
        if outs:
            places = range(len(shapes), len(shapes) + len(outs))
            line_listed.append((line.sums, slot(line.value), slot(line.got), places))
            shapes += outs
        counts.append(len(outs))
    if not shapes:
        return []
    first_out = len(arrays) + len(after)
    jobs = [job[:5] + (first_out + job[5],) for job in listed]
    line_jobs = [job[:3] + ([first_out + i for i in job[3]],) for job in line_listed]
    outs = pl.pallas_call(
        functools.partial(round_kernel, jobs, line_jobs),
        in_specs=[pl.BlockSpec(memory_space=pltpu.VMEM)] * len(arrays)
        + [pl.BlockSpec(memory_space=pl.ANY)] * len(after),
        out_specs=[pl.BlockSpec(memory_space=pltpu.VMEM)] * len(shapes),
        out_shape=shapes,
        compiler_params=pltpu.CompilerParams(vmem_limit_bytes=58 * 2**20),
        name="round",
    )(*arrays, *after)
    sent = []
    for fold, count in zip(list(folds) + list(lines), counts):
        sent += fold.take(outs[:count])
        outs = outs[count:]
    return sent


def finish_kernel(steps, here_ref, *refs):
    ins, (qkv_ref, proj_ref, up_ref, down_ref, back_ref, at_ref, ff_ref) = refs[:-7], refs[-7:]
    rows, width = proj_ref.shape[1:]
    ins, parts = ins[: 2 * SLABS * LAYERS], ins[2 * SLABS * LAYERS :]
    for step, part in zip(steps, parts):
        back_ref[jnp.bitwise_xor(here_ref[0], step)] = part[...]
    for layer in range(LAYERS):
        at, ff = ins[:SLABS], ins[SLABS : 2 * SLABS]
        ins = ins[2 * SLABS :]
        for step in range(SLABS):
            place = jnp.bitwise_xor(here_ref[1], step)
            at_ref[place] = at[step][0]
            ff_ref[place] = ff[step][...]
        for place in range(SLABS):
            cols = slice(place * width, (place + 1) * width)
            if place < 3:
                qkv_ref[layer, :, cols] = at_ref[place].astype(wide)
            else:
                proj_ref[layer] = at_ref[place].astype(wide)
            up_ref[layer, :, cols] = ff_ref[place, 0].astype(wide)
            down_ref[layer, place * rows : (place + 1) * rows] = ff_ref[place, 1].astype(wide)


def finish(here, owned, back, steps):
    arrays = [part for at, ff in owned for part in (*at, *ff)] + back
    rows, width = owned[0][0][0].shape[1:]
    outs = [
        shape_of((LAYERS, rows, 3 * width), wide),
        shape_of((LAYERS, rows, width), wide),
        shape_of((LAYERS, rows, SLABS * width), wide),
        shape_of((LAYERS, SLABS * rows, width), wide),
        shape_of((len(back),) + back[0].shape, wide),
    ]
    return pl.pallas_call(
        functools.partial(finish_kernel, steps),
        grid_spec=pltpu.PrefetchScalarGridSpec(
            num_scalar_prefetch=1,
            grid=(1,),
            in_specs=[full(part.shape) for part in arrays],
            out_specs=[full(out.shape) for out in outs],
            scratch_shapes=[
                pltpu.VMEM((SLABS, rows, width), low_type),
                pltpu.VMEM((SLABS, 2, rows, width), low_type),
            ],
        ),
        out_shape=outs,
        compiler_params=pltpu.CompilerParams(vmem_limit_bytes=58 * 2**20),
        name="finish",
    )(here, *arrays)


def finish_plain(here, owned, places):
    found = [[], [], [], []]
    order = jnp.bitwise_xor(jnp.arange(places, dtype=jnp.int32), here[1])
    for at, ff in owned:
        at = jnp.take(jnp.stack(at), order, axis=0)[:, 0].astype(wide)
        ff = jnp.take(jnp.stack(ff), order, axis=0).transpose(1, 0, 2, 3).astype(wide)
        width = at.shape[-1]
        at = at.reshape(SLABS, -1, width)
        ff = ff.reshape(2, SLABS, -1, width)
        rows = at.shape[1]
        found[0].append(at[:3].transpose(1, 0, 2).reshape(rows, 3 * width))
        found[1].append(at[3])
        found[2].append(ff[0].transpose(1, 0, 2).reshape(rows, SLABS * width))
        found[3].append(ff[1].reshape(SLABS * rows, width))
    return [jnp.stack(each) for each in found]


def place_kernel(here_ref, own_ref, own_far_ref, *refs):
    near, far, out_ref = refs[:4], refs[4:8], refs[8]
    replica = here_ref[1]
    pair = pl.program_id(0) // 2
    odd = pl.program_id(0) % 2
    half = out_ref.shape[3] // 2
    for parity, own, parts in ((0, own_ref, near), (1, own_far_ref, far)):

        @pl.when(jnp.logical_and(pair == 0, odd == parity))
        def _():
            for place in range(SLABS):
                out_ref[place, 0] = own[place]

        @pl.when(jnp.logical_and(pair > 0, odd == parity))
        def _():
            for part, steps, low in zip(parts, ((0, 1), (2, 3), (0, 2), (1, 3)), (0, 0, half, half)):
                for i, step in enumerate(steps):
                    place = jnp.bitwise_xor(replica, step)
                    for k in range(out_ref.shape[2]):
                        out_ref[place, 0, k, low : low + half] = part[i, 0, k]


def place_weights(net, here, own, own_far, near, far):
    places, kinds, rows, width = own.shape
    half = rows // 2
    whole = pl.BlockSpec(own.shape, lambda g, here_ref: (0, 0, 0, 0))
    part = pl.BlockSpec(
        (2, 1, kinds, half, width),
        lambda g, here_ref: (0, jnp.maximum(g // 2 - 1, 0), 0, 0, 0),
    )

    def target(g, here_ref):
        pair = g // 2
        step = (pair % 2) * 4 + (pair // 2) * 2 + g % 2
        return (0, jnp.bitwise_xor(here_ref[0], step), 0, 0, 0)

    return pl.pallas_call(
        place_kernel,
        grid_spec=pltpu.PrefetchScalarGridSpec(
            num_scalar_prefetch=1,
            grid=(net.shards,),
            in_specs=[whole, whole] + [part] * 8,
            out_specs=pl.BlockSpec((places, 1, kinds, rows, width), target),
        ),
        out_shape=shape_of((places, net.shards, kinds, rows, width), low_type),
        compiler_params=pltpu.CompilerParams(vmem_limit_bytes=56 * 2**20),
        name="place_weights",
    )(here, own, own_far, *near, *far)


def gather_steps(net, here, packed):
    own_far = net.swap(packed, "shard", 1)
    mine = lax.dynamic_index_in_dim(packed, here[1], 0, keepdims=True)
    got = net.swap(mine, "shard", 4)
    yield [mine]
    both = jnp.concatenate([mine, got])
    more = net.swap(both, "shard", 2)
    yield [both]
    half = packed.shape[2] // 2
    halves = []
    for cut in (slice(0, half), slice(half, None)):
        halves.append(jnp.concatenate([got[:, :, cut], more[:, :, cut]])[None])
    gots = [net.swap(part, "replica", step) for part, step in zip(halves, (1, 2))]
    yield halves
    firsts = [jnp.concatenate([part, came]) for part, came in zip(halves, gots)]
    seconds = [net.swap(part, "replica", step) for part, step in zip(firsts, (2, 1))]
    firsts_far = [net.swap(part, "shard", 1) for part in firsts]
    yield firsts
    seconds_far = [net.swap(part, "shard", 1) for part in seconds]
    yield seconds
    near = [firsts[0], seconds[0], firsts[1], seconds[1]]
    far = [firsts_far[0], seconds_far[0], firsts_far[1], seconds_far[1]]
    return place_weights(net, here, packed, own_far, near, far)


def gather_whole(net, here, packed):
    mine = lax.dynamic_index_in_dim(packed, here[1], 0, keepdims=False)
    flat = mine.reshape(-1, mine.shape[-1])
    whole = lax.all_gather(flat, ("replica", "shard"), axis=0, tiled=True)
    return whole.reshape((net.replicas, net.shards) + mine.shape)


def plain_slabs(net, whole, tall_kind):
    places, shards, kinds, part, width = whole.shape
    split = whole.reshape(SLABS, places // SLABS, shards, kinds, part, width)
    split = split.transpose(3, 0, 2, 1, 4, 5).reshape(kinds, SLABS, shards, -1, width)
    made = []
    for kind in range(kinds):
        each = split[kind]
        if kind == tall_kind:
            each = each.transpose(1, 0, 2, 3)
        made.append(each.reshape(SLABS, 1, width, width))
    return jnp.stack(made, axis=2)


class Steps:
    def __init__(self, steps):
        self.steps = steps
        self.result = None
        self.over = False

    def go(self, count=1):
        sent = []
        for _ in range(count):
            if not self.over:
                try:
                    sent = next(self.steps)
                except StopIteration as end:
                    self.over = True
                    self.result = end.value
                    sent = []
        return list(sent)

    def end(self):
        while not self.over:
            self.go()
        return self.result


def local(
    net,
    hidden_in,
    condition,
    latent_live,
    out_grad,
    ada_weight,
    qkv_weight,
    proj_weight,
    fc1_weight,
    fc2_weight,
    ada_bias,
    qv_bias,
    proj_bias,
    fc1_bias,
    fc2_bias,
):
    shard = lax.axis_index("shard")
    replica = lax.axis_index("replica")
    here = jnp.stack([shard, replica]).astype(jnp.int32)
    shards, replicas = net.shards, net.replicas
    latents_here, model_width = condition.shape
    rows = proj_weight.shape[1]
    piece_rows = rows * SLABS // replicas
    mod_width = ada_weight.shape[2]

    fused = replicas == SLABS and shards == 2 * SLABS and rows % 16 == 0

    def pack(layer):
        qkv = qkv_weight[layer].astype(low_type)
        up = fc1_weight[layer].astype(low_type)
        down = fc2_weight[layer].astype(low_type)
        columns = lambda w, b: w[:, b * model_width : (b + 1) * model_width]
        attn = [columns(qkv, b) for b in range(3)] + [proj_weight[layer].astype(low_type)]
        kinds = [jnp.stack(attn), jnp.stack([columns(up, b) for b in range(SLABS)]), down]
        return [kind.reshape(replicas, 1, piece_rows, model_width) for kind in kinds]

    packs = [pack(layer) for layer in range(LAYERS)]
    if fused:
        a0 = Steps(gather_steps(net, here, packs[0][0]))
        later = gather_whole(net, here, jnp.concatenate(packs[1] + packs[0][1:], axis=1))
    else:
        wholes = [
            plain_slabs(net, gather_whole(net, here, jnp.concatenate(kinds, axis=1)), 2)
            for kinds in packs
        ]

    cond_low = jax.nn.silu(condition).astype(low_type)
    bias_rows = jnp.concatenate([qv_bias, proj_bias, fc1_bias, fc2_bias], axis=1).astype(low_type)
    bias_width = bias_rows.shape[1]
    bias_rows = jnp.pad(bias_rows, ((0, 0), (0, model_width - bias_width)))
    both_rel = net.gather_rel(jnp.concatenate([cond_low, bias_rows]), ["shard"])
    cond_rel = both_rel[:, :latents_here]
    found = net.order("shard")
    spots = jnp.array([found.index(step) for step in range(shards)], jnp.int32)
    order = jnp.take(spots, jnp.bitwise_xor(jnp.arange(shards, dtype=jnp.int32), here[0]))
    bias_all = jnp.take(both_rel[:, latents_here:], order, axis=0)
    group = shards * latents_here
    cond_line = Line(net, cond_rel.reshape(1, group, model_width), ["replica"])
    cond_rows = lax.dynamic_slice_in_dim(
        cond_rel.reshape(group, model_width), shard * rows, rows, axis=1
    )
    ada_low = ada_weight.astype(low_type)
    partial = jnp.stack([nn(cond_rows, ada_low[layer]) for layer in range(LAYERS)], axis=1)
    ada_part = ada_bias.shape[1]
    bias_here = lax.dynamic_update_slice_in_dim(
        jnp.zeros((LAYERS, mod_width), wide),
        ada_bias.astype(low_type).astype(wide),
        shard * ada_part,
        axis=1,
    )
    partial = (partial + bias_here[None]).reshape(shards, latents_here, LAYERS, mod_width)
    modulations = net.scatter_rel(partial)

    widths = (qv_bias.shape[1], proj_bias.shape[1], fc1_bias.shape[1], fc2_bias.shape[1])
    starts = (0, widths[0], widths[0] + widths[1], widths[0] + widths[1] + widths[2])

    def biases_of(layer):
        qv, proj, up, down = [
            bias_all[:, layer, start : start + width].reshape(-1).astype(wide)
            for start, width in zip(starts, widths)
        ]
        qkv_b = jnp.stack([qv[:model_width], jnp.zeros((model_width,), wide), qv[model_width:]])
        up_b = up.reshape(SLABS, 1, model_width)
        return (qkv_b[:, None], proj[None], up_b, down[None])

    def attn_first():
        return (a0.end(), 0), []

    if fused:
        attn_calls = (attn_first, lambda: ((later, 0), []))
        feed_calls = (
            lambda: ((later, 3), (later, 4), []),
            lambda: ((later, 1), (later, 2), []),
        )
        slot_calls = [lambda: []] * LAYERS
    else:
        attn_calls = [lambda w=w: ((w, 0), []) for w in wholes]
        feed_calls = [lambda w=w: ((w, 1), (w, 2), []) for w in wholes]
        slot_calls = [lambda: []] * LAYERS

    live_rows = latent_live.astype(wide)[:, None, None]
    saved_all = []
    current = hidden_in
    weights_all = []
    for layer in range(LAYERS):
        current, saved_state, layer_weights = forward_layer(
            here,
            current,
            modulations[:, layer].reshape(latents_here, 6, model_width),
            attn_calls[layer],
            feed_calls[layer],
            biases_of(layer),
            slot_calls[layer],
        )
        saved_all.append(saved_state)
        weights_all.append(layer_weights)
    result = current * live_rows
    grad_now = out_grad * live_rows

    def send(grads, lazy):
        if fused:
            return Fold(net, list(zip(grads[::2], grads[1::2])), lazy)
        slabs = [grads[0].reshape(SLABS, shards, rows, model_width)]
        if len(grads) > 1:
            down = grads[1].reshape(shards, SLABS, rows, model_width)
            slabs.append(down.transpose(1, 0, 2, 3))
        pairs = [[half[0] for half in order_grads(net, here, each)] for each in slabs]
        return Steps(reduce_steps(net, here, pairs))

    sends = {}
    bias_line = [None]

    def bias_row(layer, sums, up_sums, down_sums):
        grads = (
            jnp.concatenate([sums[0], sums[2]]),
            sums[3],
            up_sums.reshape(-1),
            down_sums[0],
        )
        bias_sums[layer] = jnp.concatenate([grad.reshape(shards, -1) for grad in grads], axis=1)
        if layer == 0:
            bias_line[0] = Line(net, jnp.stack(bias_sums), ["shard", "replica"], sums=True)

    def middle_slot(layer):
        def slot(ff_grads):
            fold = sends["ff", layer] = send(ff_grads, layer == 0)
            if not fused:
                return []
            if layer == 1:
                return fold.sent
            return run_round([sends["ff", 1], sends["at", 1], fold])

        return slot

    def late_slot(layer):
        def slot(sums, up_sums, down_sums):
            bias_row(layer, sums, up_sums, down_sums)
            if not fused:
                return []
            if layer == 1:
                return run_round([sends["ff", 1]], [cond_line])
            return bias_line[0].sent + run_round([sends["ff", 1], sends["at", 1], sends["ff", 0]])

        return slot

    ada_wide = ada_low.astype(wide)
    grad_cond = jnp.zeros((group, rows), wide)
    ada_grads = [None] * LAYERS
    modul_grads = [None] * LAYERS
    bias_sums = [None] * LAYERS
    for layer in reversed(range(LAYERS)):
        before = []
        if layer == 0 and fused:
            before = run_round([sends["ff", 1], sends["at", 1]], [cond_line])
        grad_now, grad_modul, at_grads = backward_layer(
            here,
            fused,
            grad_now,
            weights_all[layer],
            saved_all[layer],
            before,
            middle_slot(layer),
            late_slot(layer),
        )
        sends["at", layer] = send(at_grads, True)
        modul_grads[layer] = grad_modul
    lines = [
        bias_line[0],
        cond_line,
        Line(
            net,
            jnp.concatenate(modul_grads)[None],
            ["shard", "replica"],
            lower_at=len(net.bits("shard")),
        ),
    ]
    if fused:
        ring = [sends["ff", 1], sends["at", 1], sends["ff", 0], sends["at", 0]]
        while any(fold.every is None for fold in ring) or not all(line.over for line in lines):
            run_round(ring, lines)
    bias_total, cond_all, modul_low = [line.end() for line in lines]
    modul = lines[2].full
    modul_low = modul_low.reshape((replicas, shards) + modul_low.shape[1:])
    cond_every = lax.dynamic_slice_in_dim(
        cond_all.reshape(replicas * group, model_width), shard * rows, rows, axis=1
    )
    per_layer = lambda w, layer: w[..., layer * latents_here : (layer + 1) * latents_here, :]
    for layer in range(LAYERS):
        mine = per_layer(modul, layer).reshape(group, mod_width)
        grad_cond = grad_cond + exact_trail(mine, ada_wide[layer])
        every = per_layer(modul_low, layer).reshape(replicas * group, mod_width)
        ada_grads[layer] = tn(cond_every, every)
    own_mod = lax.dynamic_slice_in_dim(modul_low, shard * ada_part, ada_part, axis=3).astype(wide)
    own_mod = own_mod.reshape(replicas * shards, LAYERS, latents_here, ada_part)
    ada_bias_out = jnp.sum(own_mod, axis=(0, 2))
    bias_mine = lax.dynamic_index_in_dim(bias_total, shard, 1, keepdims=False)
    bias_out = [bias_mine[:, start : start + width] for start, width in zip(starts, widths)]

    parts = grad_cond.reshape(shards, latents_here, rows)
    back = [parts[0]]
    back += [net.swap(parts[i], "shard", found[i]) for i in range(1, shards)]
    if fused:
        owned = [(sends["at", layer].every, sends["ff", layer].every) for layer in range(LAYERS)]
        *weight_outs, back = finish(here, owned, back, found)
    else:
        owned = [
            (sends["at", layer].end(), sends["ff", layer].end()) for layer in range(LAYERS)
        ]
        weight_outs = finish_plain(here, owned, replicas)
        back = jnp.take(jnp.stack(back), order, axis=0)
    cond_back = back.transpose(1, 0, 2).reshape(latents_here, model_width)
    grad_condition = jax.vjp(jax.nn.silu, condition)[1](cond_back)[0]
    return (
        result,
        grad_now,
        grad_condition,
        jnp.stack(ada_grads),
        *weight_outs,
        ada_bias_out,
        *bias_out,
    )


def solution(mesh):
    tokens = P(("replica", "shard"), None, None)
    weight = P(None, "shard", None)
    bias = P(None, "shard")
    rows = P(("replica", "shard"), None)
    return jax.shard_map(
        functools.partial(local, Net(mesh)),
        mesh=mesh,
        in_specs=(tokens, rows, P(("replica", "shard")), tokens) + (weight,) * 5 + (bias,) * 5,
        out_specs=(tokens, tokens, rows) + (weight,) * 5 + (bias,) * 5,
        check_vma=False,
    )
```

```python
import functools

import jax
import jax.numpy as jnp
from jax import lax
from jax.experimental import pallas as pl
from jax.experimental.pallas import tpu as pltpu
from jax.sharding import PartitionSpec as P

HEADS = 12
HEAD_DIM = 64
LAYERS = 2
SLABS = 4

norm_eps = 1e-06
highest = lax.Precision.HIGHEST
low_type = jnp.bfloat16
wide = jnp.float32


def nn(left, right):
    return lax.dot_general(left, right, (((1,), (0,)), ((), ())), preferred_element_type=wide)


def nt(left, right):
    return lax.dot_general(left, right, (((1,), (1,)), ((), ())), preferred_element_type=wide)


def tn(left, right):
    return lax.dot_general(left, right, (((0,), (0,)), ((), ())), preferred_element_type=wide)


def exact_lead(left_side, right_side):
    return lax.dot_general(
        left_side,
        right_side,
        (((0,), (0,)), ((), ())),
        precision=highest,
        preferred_element_type=wide,
    )


def exact_trail(left_side, right_side):
    return lax.dot_general(
        left_side,
        right_side,
        (((1,), (1,)), ((), ())),
        precision=highest,
        preferred_element_type=wide,
    )


def normalise(rows):
    centred = rows - jnp.mean(rows, axis=-1, keepdims=True)
    spread = jnp.mean(centred * centred, axis=-1, keepdims=True)
    inverse = lax.rsqrt(spread + norm_eps)
    return centred * inverse, inverse


def norm_back(grad, rows, stretch):
    normed, inverse = normalise(rows)
    inner = grad * (1.0 + stretch)
    first = jnp.mean(inner, axis=-1, keepdims=True)
    second = jnp.mean(inner * normed, axis=-1, keepdims=True)
    back = (inner - first - normed * second) * inverse
    return (
        back,
        jnp.sum(grad, axis=0, keepdims=True),
        jnp.sum(grad * normed, axis=0, keepdims=True),
    )


def slab(ref):
    return ref[0].reshape(ref.shape[3], ref.shape[3])


def tall(ref):
    if ref.shape[0] == 1:
        return slab(ref)
    return jnp.concatenate(
        [ref[r, s] for s in range(ref.shape[1]) for r in range(ref.shape[0])], axis=0
    )


def qkv_kernel(x_ref, mod_ref, w_ref, b_ref, u_ref, qkv_ref):
    latents, seq, _ = x_ref.shape

    @pl.when(pl.program_id(0) == 0)
    def _():
        for i in range(latents):
            normed, _ = normalise(x_ref[i])
            u_ref[i * seq : (i + 1) * seq] = (
                normed * (1.0 + mod_ref[i, 1:2]) + mod_ref[i, 0:1]
            ).astype(low_type)

    for i in range(latents):
        part = slice(i * seq, (i + 1) * seq)
        qkv_ref[0, part] = (nn(u_ref[part], slab(w_ref)) + b_ref[0]).astype(low_type)


def mix_kernel(qkv_ref, x_ref, mod_ref, w_ref, b_ref, o_ref, a_ref, x1_ref, u2_ref):
    seq, width = o_ref.shape
    pair = 2 * HEAD_DIM
    lane = lax.broadcasted_iota(jnp.int32, (seq, pair), 1)
    left = lane < HEAD_DIM
    for at in range(0, width, pair):
        query = qkv_ref[0, :, at : at + pair]
        key = qkv_ref[1, :, at : at + pair]
        value = qkv_ref[2, :, at : at + pair]
        mixed = []
        for side in (left, jnp.logical_not(left)):
            raw = nt(jnp.where(side, query, jnp.zeros_like(query)), key) * HEAD_DIM ** (-0.5)
            top = jnp.exp(raw - jnp.max(raw, axis=-1, keepdims=True))
            probs = top * (1.0 / jnp.sum(top, axis=-1, keepdims=True))
            mixed.append(nn(probs.astype(low_type), value))
        o_ref[:, at : at + pair] = jnp.where(left, mixed[0], mixed[1]).astype(low_type)
    branch = nn(o_ref[...], slab(w_ref)) + b_ref[...]
    a_ref[...] = branch
    middle = x_ref[0] + mod_ref[0, 2:3] * branch
    x1_ref[...] = middle
    normed, _ = normalise(middle)
    u2_ref[...] = (normed * (1.0 + mod_ref[0, 4:5]) + mod_ref[0, 3:4]).astype(low_type)


GELU_SCALE = 0.7978845608028654
GELU_CUBE = 0.044715


def feed_kernel(
    u2_ref, x1_ref, mod_ref, up_ref, upb_ref, down_ref, downb_ref, g_ref, slope_ref, m_ref, x_ref
):
    latents = mod_ref.shape[0]
    seq = u2_ref.shape[0] // latents
    step = pl.program_id(0)
    down = tall(down_ref)
    for i in range(latents):
        part = slice(i * seq, (i + 1) * seq)
        pre = nn(u2_ref[part], slab(up_ref)) + upb_ref[0]
        square = pre * pre
        bent = jnp.tanh(GELU_SCALE * (pre + GELU_CUBE * (square * pre)))
        half = 0.5 * (1.0 + bent)
        act = (pre * half).astype(low_type)
        g_ref[0, part] = act
        slope_ref[0, part] = (
            half
            + (0.5 * GELU_SCALE)
            * pre
            * (1.0 - bent * bent)
            * (1.0 + (3.0 * GELU_CUBE) * square)
        ).astype(low_type)
        part_sum = nn(act, down)

        @pl.when(step == 0)
        def _():
            m_ref[part] = part_sum + downb_ref[...]

        @pl.when(step > 0)
        def _():
            m_ref[part] = m_ref[part] + part_sum

        @pl.when(step == pl.num_programs(0) - 1)
        def _():
            x_ref[part] = x1_ref[part] + mod_ref[i, 5:6] * m_ref[part]


def store_slab(here_ref, product, kept_ref, sent_ref, hold_ref):
    hold_ref[...] = product.astype(low_type).reshape(hold_ref.shape)
    for near in range(kept_ref.shape[0]):
        owner = jnp.bitwise_xor(here_ref[0], 2 * near)
        kept_ref[near, 0] = hold_ref[owner]
        sent_ref[near, 0] = hold_ref[jnp.bitwise_xor(owner, 1)]


def feed_back_kernel(
    fused, here_ref, dy_ref, m_ref, mod_ref, u2_ref, g_ref, slope_ref, up_ref, down_ref,
    *refs,
):
    if fused:
        up_grads, down_grads, refs = refs[:2], refs[2:4], refs[4:]
    else:
        up_grad, down_grad, refs = refs[0], refs[1], refs[2:]
    du_ref, dgate_ref, downb_ref, upb_ref, dm_ref, df_ref, hold_ref = refs
    latents = mod_ref.shape[0]
    seq = u2_ref.shape[0] // latents
    step = pl.program_id(0)

    @pl.when(step == 0)
    def _():
        total = jnp.zeros(downb_ref.shape, wide)
        for i in range(latents):
            part = slice(i * seq, (i + 1) * seq)
            grad = dy_ref[part]
            dgate_ref[i] = jnp.sum(grad * m_ref[part], axis=0, keepdims=True)
            lower = (grad * mod_ref[i, 5:6]).astype(low_type)
            dm_ref[part] = lower
            total += jnp.sum(lower.astype(wide), axis=0, keepdims=True)
        downb_ref[...] = total

    sums = jnp.zeros(upb_ref.shape[1:], wide)
    down = tall(down_ref)
    for i in range(latents):
        part = slice(i * seq, (i + 1) * seq)
        lower = (nt(dm_ref[part], down) * slope_ref[0, part].astype(wide)).astype(low_type)
        df_ref[part] = lower
        sums += jnp.sum(lower.astype(wide), axis=0, keepdims=True)
        back = nt(lower, slab(up_ref))

        @pl.when(step == 0)
        def _():
            du_ref[part] = back

        @pl.when(step > 0)
        def _():
            du_ref[part] = du_ref[part] + back

    upb_ref[0] = sums
    down_part = tn(g_ref[0], dm_ref[...])
    up_part = tn(u2_ref[...], df_ref[...])
    if not fused:
        down_grad[0] = down_part.astype(low_type)
        up_grad[0] = up_part.astype(low_type)
        return
    store_slab(here_ref, up_part, up_grads[0], up_grads[1], hold_ref)
    hold_ref[...] = down_part.astype(low_type).reshape(hold_ref.shape)
    places = down_grads[0].shape[1]
    low = here_ref[0] % 2
    for place in range(places):
        piece = jnp.bitwise_xor(here_ref[1], place)
        down_grads[0][0, place] = hold_ref[low * places + piece]
        down_grads[1][0, place] = hold_ref[(1 - low) * places + piece]


def mix_back_kernel(
    du_ref, x1_ref, dy_ref, a_ref, qkv_ref, mod_ref, w_ref,
    dx1_ref, dall_ref, dmod_ref, sums_ref, do_ref,
):
    seq, width = x1_ref.shape
    pair = 2 * HEAD_DIM
    back, dshift, dscale = norm_back(du_ref[...], x1_ref[...], mod_ref[0, 4:5])
    dx1 = back + dy_ref[...]
    dx1_ref[...] = dx1
    dmod_ref[0, 0:1] = dshift
    dmod_ref[0, 1:2] = dscale
    dmod_ref[0, 2:3] = jnp.sum(dx1 * a_ref[...], axis=0, keepdims=True)
    da = (dx1 * mod_ref[0, 2:3]).astype(low_type)
    dall_ref[3] = da
    do_ref[...] = nt(da, slab(w_ref)).astype(low_type)
    lane = lax.broadcasted_iota(jnp.int32, (seq, pair), 1)
    left = lane < HEAD_DIM
    for at in range(0, width, pair):
        cols = slice(at, at + pair)
        query = qkv_ref[0, :, cols]
        key = qkv_ref[1, :, cols]
        value = qkv_ref[2, :, cols]
        grad = do_ref[:, cols]
        found = []
        for side in (left, jnp.logical_not(left)):
            none = jnp.zeros_like(query)
            raw = nt(key, jnp.where(side, query, none)) * HEAD_DIM ** (-0.5)
            top = jnp.exp(raw - jnp.max(raw, axis=0, keepdims=True))
            probs = top * (1.0 / jnp.sum(top, axis=0, keepdims=True))
            dvalue = nn(probs.astype(low_type), grad)
            dprobs = nt(value, jnp.where(side, grad, none))
            dots = jnp.sum(dprobs * probs, axis=0, keepdims=True)
            draw = (probs * (dprobs - dots) * HEAD_DIM ** (-0.5)).astype(low_type)
            found.append((tn(draw, key), nn(draw, query), dvalue))
        for which in range(3):
            dall_ref[which, :, cols] = jnp.where(
                left, found[0][which], found[1][which]
            ).astype(low_type)

    @pl.when(pl.program_id(0) == 0)
    def _():
        sums_ref[...] = jnp.zeros_like(sums_ref)

    for which in range(4):
        sums_ref[which : which + 1] += jnp.sum(
            dall_ref[which].astype(wide), axis=0, keepdims=True
        )


def qkv_back_kernel(
    fused, here_ref, u1_ref, o_ref, dall_ref, w_ref, x_ref, dx1_ref, mod_ref, *refs
):
    grads = refs[:2] if fused else refs[:1]
    dx_ref, dmod_ref, acc_ref, hold_ref = refs[len(grads) :]

    def store(product):
        if fused:
            store_slab(here_ref, product, grads[0], grads[1], hold_ref)
        else:
            grads[0][0] = product.astype(low_type)

    latents, seq, _ = x_ref.shape
    step = pl.program_id(0)

    @pl.when(step < 3)
    def _():
        store(tn(u1_ref[...], dall_ref[0]))
        for i in range(latents):
            part = slice(i * seq, (i + 1) * seq)
            back = nt(dall_ref[0, part], slab(w_ref))

            @pl.when(step == 0)
            def _():
                acc_ref[part] = back

            @pl.when(step > 0)
            def _():
                acc_ref[part] = acc_ref[part] + back

    @pl.when(step == 3)
    def _():
        store(tn(o_ref[...], dall_ref[0]))
        for i in range(latents):
            part = slice(i * seq, (i + 1) * seq)
            back, dshift, dscale = norm_back(acc_ref[part], x_ref[i], mod_ref[i, 1:2])
            dx_ref[i] = back + dx1_ref[part]
            dmod_ref[i, 0:1] = dshift
            dmod_ref[i, 1:2] = dscale


def shape_of(dims, kind):
    return jax.ShapeDtypeStruct(tuple(dims), kind)


def full(dims):
    return pl.BlockSpec(tuple(dims), lambda step, here_ref: (0,) * len(dims))


def along(dims, where):
    return pl.BlockSpec(
        tuple(dims),
        lambda step, here_ref: tuple(step if i == where else 0 for i in range(len(dims))),
    )


def slab_spec(weight, fixed=None):
    array, kind = weight
    _, shards, _, rows, width = array.shape
    return pl.BlockSpec(
        (1, shards, None, rows, width),
        lambda step, here_ref: (step if fixed is None else fixed, 0, kind, 0, 0),
    )


def tall_spec(weight):
    array, kind = weight
    slabs, shards, _, rows, width = array.shape
    if shards == 1:
        return slab_spec(weight)
    return pl.BlockSpec(
        (slabs, shards // slabs, None, rows, width), lambda step, here_ref: (0, step, kind, 0, 0)
    )


def call(
    kernel, here, grid, in_specs, out_specs, out_shape, scratch, flops, moved, after=(), fused=None
):
    count = len(in_specs)

    def body(here_ref, *refs):
        lead = () if fused is None else (fused, here_ref)
        kernel(*lead, *refs[:count], *refs[count + len(after) :])

    run = pl.pallas_call(
        body,
        grid_spec=pltpu.PrefetchScalarGridSpec(
            num_scalar_prefetch=1,
            grid=(grid,),
            in_specs=list(in_specs) + [pl.BlockSpec(memory_space=pl.ANY)] * len(after),
            out_specs=out_specs,
            scratch_shapes=scratch,
        ),
        out_shape=out_shape,
        compiler_params=pltpu.CompilerParams(vmem_limit_bytes=58 * 2**20),
        cost_estimate=pl.CostEstimate(flops=flops, bytes_accessed=moved, transcendentals=0),
        name=kernel.__name__,
    )
    return lambda *arrays: run(here, *arrays, *after)


def forward_layer(here, hidden, mod, attn, feed, biases, slots):
    qkv_b, proj_b, up_b, down_b = biases
    attn_w, after = attn()
    latents, seq, width = hidden.shape
    rows = latents * seq
    unit = 2 * rows * width * width
    size = rows * width
    u1, qkv = call(
        qkv_kernel,
        here,
        3,
        [
            full(hidden.shape),
            full(mod.shape),
            slab_spec(attn_w),
            along((1, 1, width), 0),
        ],
        [full((rows, width)), along((1, rows, width), 0)],
        [shape_of((rows, width), low_type), shape_of((3, rows, width), low_type)],
        [],
        3 * unit,
        18 * size,
        after,
    )(hidden, mod, attn_w[0], qkv_b)
    token = along((seq, width), 0)
    mixed, branch, middle, u2 = call(
        mix_kernel,
        here,
        latents,
        [
            along((3, seq, width), 1),
            along((1, seq, width), 0),
            along((1, 6, width), 0),
            slab_spec(attn_w, 3),
            full((1, width)),
        ],
        [token, token, token, token],
        [
            shape_of((rows, width), low_type),
            shape_of((rows, width), wide),
            shape_of((rows, width), wide),
            shape_of((rows, width), low_type),
        ],
        [],
        5 * unit,
        24 * size,
        slots(),
    )(qkv, hidden, mod, attn_w[0], proj_b)
    up_w, down_w, after = feed()
    act, slope, branch_two, result = call(
        feed_kernel,
        here,
        SLABS,
        [
            full((rows, width)),
            full((rows, width)),
            full(mod.shape),
            slab_spec(up_w),
            along((1, 1, width), 0),
            tall_spec(down_w),
            full((1, width)),
        ],
        [
            along((1, rows, width), 0),
            along((1, rows, width), 0),
            full((rows, width)),
            full((rows, width)),
        ],
        [
            shape_of((SLABS, rows, width), low_type),
            shape_of((SLABS, rows, width), low_type),
            shape_of((rows, width), wide),
            shape_of((rows, width), wide),
        ],
        [],
        12 * unit,
        40 * size,
        after,
    )(u2, middle, mod, up_w[0], up_b, down_w[0], down_b)
    saved = (hidden, mod, u1, qkv, mixed, branch, middle, u2, act, slope, branch_two)
    return result.reshape(hidden.shape), saved, (attn_w, up_w, down_w)


def backward_layer(here, fused, grad_out, weights, saved, before, middle_slot, late_slot):
    attn_w, up_w, down_w = weights
    hidden, mod, u1, qkv, mixed, branch, middle, u2, act, slope, branch_two = saved
    latents, seq, width = hidden.shape
    rows = latents * seq
    unit = 2 * rows * width * width
    size = rows * width
    grad_out = grad_out.reshape(rows, width)
    block = along((1, rows, width), 0)
    flat = full((rows, width))
    square = along((1, width, width), 0)
    _, shards, _, own, _ = attn_w[0].shape
    near = shards // 2
    by_place = pl.BlockSpec(
        (near, 1, own, width),
        lambda step, here_ref: (0, jnp.bitwise_xor(here_ref[1], step), 0, 0),
    )
    by_near = pl.BlockSpec(
        (1, SLABS, own, width),
        lambda step, here_ref: (jnp.bitwise_xor(here_ref[0] // 2, step), 0, 0, 0),
    )
    half = shape_of((near, SLABS, own, width), low_type)
    natural = shape_of((SLABS, width, width), low_type)
    hold = pltpu.VMEM((shards, own, width), low_type)
    *ff_grads, du2, dgate_two, down_sums, up_sums = call(
        feed_back_kernel,
        here,
        SLABS,
        [flat, flat, full(mod.shape), flat, block, block, slab_spec(up_w), tall_spec(down_w)],
        ([by_place, by_place, by_near, by_near] if fused else [square, square])
        + [flat, full((latents, 1, width)), full((1, width)), along((1, 1, width), 0)],
        ([half] * 4 if fused else [natural] * 2)
        + [
            shape_of((rows, width), wide),
            shape_of((latents, 1, width), wide),
            shape_of((1, width), wide),
            shape_of((SLABS, 1, width), wide),
        ],
        [pltpu.VMEM((rows, width), low_type), pltpu.VMEM((rows, width), low_type), hold],
        16 * unit,
        50 * size,
        before,
        fused,
    )(grad_out, branch_two, mod, u2, act, slope, up_w[0], down_w[0])
    token = along((seq, width), 0)
    dx1, dall, dmod_mid, sums = call(
        mix_back_kernel,
        here,
        latents,
        [
            token,
            token,
            token,
            token,
            along((3, seq, width), 1),
            along((1, 6, width), 0),
            slab_spec(attn_w, 3),
        ],
        [
            token,
            along((4, seq, width), 1),
            along((1, 3, width), 0),
            full((4, width)),
        ],
        [
            shape_of((rows, width), wide),
            shape_of((4, rows, width), low_type),
            shape_of((latents, 3, width), wide),
            shape_of((4, width), wide),
        ],
        [pltpu.VMEM((seq, width), low_type)],
        10 * unit,
        40 * size,
        middle_slot(ff_grads),
    )(du2, middle, grad_out, branch, qkv, mod, attn_w[0])
    *at_grads, dx, dmod_low = call(
        qkv_back_kernel,
        here,
        4,
        [flat, flat, block, slab_spec(attn_w), full(hidden.shape), flat, full(mod.shape)],
        ([by_place, by_place] if fused else [square])
        + [full(hidden.shape), full((latents, 2, width))],
        ([half] * 2 if fused else [natural])
        + [shape_of(hidden.shape, wide), shape_of((latents, 2, width), wide)],
        [pltpu.VMEM((rows, width), wide), hold],
        7 * unit,
        36 * size,
        late_slot(sums, up_sums, down_sums),
        fused,
    )(u1, mixed, dall, attn_w[0], hidden, dx1, mod)
    dmod = jnp.concatenate(
        [dmod_low, dmod_mid[:, 2:3], dmod_mid[:, 0:2], dgate_two], axis=1
    ).reshape(latents, 6 * width)
    return dx, dmod, at_grads


class Net:
    def __init__(self, mesh):
        self.replicas = mesh.shape["replica"]
        self.shards = mesh.shape["shard"]

    def swap(self, values, axis, step):
        count = self.replicas if axis == "replica" else self.shards
        return lax.ppermute(values, axis, [(i, i ^ step) for i in range(count)])

    def bits(self, axis):
        count = self.replicas if axis == "replica" else self.shards
        found = []
        step = 1
        while step < count:
            found.append(step)
            step *= 2
        return found

    def gather_rel(self, values, axes):
        stack = values[None]
        for axis in axes:
            for step in self.bits(axis)[::-1]:
                stack = jnp.concatenate([stack, self.swap(stack, axis, step)])
        return stack

    def order(self, axis):
        found = [0]
        for step in self.bits(axis)[::-1]:
            found = found + [place ^ step for place in found]
        return found

    def scatter_rel(self, stack):
        for step in self.bits("shard"):
            half = stack.shape[0] // 2
            stack = stack[:half] + self.swap(stack[half:], "shard", step)
        return stack[0]


def order_kernel(places, pieces_per_slab, here_ref, near_ref, keep_ref, send_ref):
    shard_low = here_ref[0] % 2
    replica = here_ref[1]
    for place in range(places):
        piece = jnp.bitwise_xor(replica, place)
        slab = piece // pieces_per_slab
        part = piece % pieces_per_slab
        keep_ref[0, place] = near_ref[slab, shard_low, part].astype(keep_ref.dtype)
        send_ref[0, place] = near_ref[slab, 1 - shard_low, part].astype(send_ref.dtype)


def order_grads(net, here, grads):
    slabs, shards, rows, width = grads.shape
    per_slab = net.replicas // SLABS if net.replicas > SLABS else 1
    places = net.replicas
    if net.replicas < SLABS:
        raise ValueError("replicas")
    piece_rows = rows * SLABS // places
    groups = slabs // SLABS
    view = grads.reshape(groups, SLABS, shards, per_slab, piece_rows, width)
    out = jax.ShapeDtypeStruct((groups, shards // 2, places, piece_rows, width), low_type)
    spec = pl.BlockSpec(
        (None, 1, places, piece_rows, width), lambda g, j, here_ref: (g, j, 0, 0, 0)
    )
    return pl.pallas_call(
        functools.partial(order_kernel, places, per_slab),
        grid_spec=pltpu.PrefetchScalarGridSpec(
            num_scalar_prefetch=1,
            grid=(groups, shards // 2),
            in_specs=[
                pl.BlockSpec(
                    (None, SLABS, 2, per_slab, piece_rows, width),
                    lambda g, j, here_ref: (
                        g,
                        0,
                        jnp.bitwise_xor(here_ref[0] // 2, j),
                        0,
                        0,
                        0,
                    ),
                )
            ],
            out_specs=[spec, spec],
        ),
        out_shape=[out, out],
        name="order_grads",
    )(here, view)


def add_low(left, right):
    return (left.astype(wide) + right.astype(wide)).astype(low_type)


def halve(stack, dim, where):
    size = stack.shape[dim]
    shape = stack.shape[:dim] + (size // (2 * where), 2, where) + stack.shape[dim + 1 :]
    view = stack.reshape(shape)
    rest = stack.shape[:dim] + (size // 2,) + stack.shape[dim + 1 :]
    return (
        lax.index_in_dim(view, 0, dim + 1, keepdims=False).reshape(rest),
        lax.index_in_dim(view, 1, dim + 1, keepdims=False).reshape(rest),
    )


def reduce_steps(net, here, pairs):
    gots = [net.swap(give, "shard", 1) for _, give in pairs]
    yield [give for _, give in pairs]
    near, places, rows, width = pairs[0][0].shape
    single = len(pairs) == 1
    if single:
        cuts = [slice(0, near // 2), slice(near // 2, near)]
        parts = [add_low(pairs[0][0][cut], gots[0][cut]) for cut in cuts]
    else:
        parts = [add_low(keep, got) for (keep, _), got in zip(pairs, gots)]
    lefts = [list(range(places))] * 2
    for steps in zip(net.bits("replica"), net.bits("replica")[::-1]):
        splits = []
        for i, step in enumerate(steps):
            where = sum(1 for q in lefts[i] if q < step)
            splits.append(halve(parts[i], 1, where))
            lefts[i] = [q for q in lefts[i] if not q & step]
        gots = [net.swap(give, "replica", step) for (_, give), step in zip(splits, steps)]
        yield [give for _, give in splits]
        parts = [add_low(keep, got) for (keep, _), got in zip(splits, gots)]
    parts = [part[:, 0] for part in parts]
    steps = net.bits("shard")[1:]
    for step in steps[:-1] if single else steps:
        splits = [halve(part, 0, 1) for part in parts]
        gots = [net.swap(give, "shard", step) for _, give in splits]
        yield [give for _, give in splits]
        parts = [add_low(keep, got) for (keep, _), got in zip(splits, gots)]
    if single:
        got = net.swap(parts[1], "shard", steps[-1])
        yield [parts[1]]
        mine = add_low(parts[0], got)
    else:
        mine = jnp.concatenate(parts)
    every = [mine] + [net.swap(mine, "replica", step) for step in range(1, places)]
    yield [mine]
    return every


class Part:
    def __init__(self, keep, labels, route):
        self.keep = keep
        self.got = None
        self.labels = labels
        self.route = route


class Fold:
    def __init__(self, net, pairs, lazy):
        self.net = net
        near, places, rows, width = pairs[0][0].shape
        ahead = [("replica", step) for step in net.bits("replica")]
        behind = ahead[::-1]
        shard_route = [("shard", step) for step in net.bits("shard")[1:]]
        flat = (near * places, rows, width)
        keeps = [keep.reshape(flat) for keep, _ in pairs]
        gives = [give.reshape(flat) for _, give in pairs]
        self.lazy = lazy
        self.gives = gives
        self.sent = [] if lazy else gives
        self.gots = [None if lazy else net.swap(give, "shard", 1) for give in gives]
        labels = [(2 * t, q) for t in range(near) for q in range(places)]
        self.single = len(pairs) == 1
        if self.single:
            half = len(labels) // 2
            self.parts = [
                Part((keeps[0], 0), labels[:half], ahead + shard_route[:-1]),
                Part((keeps[0], half), labels[half:], behind + shard_route[:-1]),
            ]
            self.last = shard_route[-1]
            starts = (0, half)
        else:
            self.parts = [
                Part((keeps[0], 0), labels, ahead + shard_route),
                Part((keeps[1], 0), labels, behind + shard_route),
            ]
            starts = (0, 0)
        self.starts = starts
        self.every = None
        self.merge = False
        self.arm()

    def arm(self):
        gots = self.gots * 2 if self.single else self.gots
        for part, got, start in zip(self.parts, gots, self.starts):
            part.got = (got, start)

    def jobs(self):
        if self.every is not None:
            return [], []
        first = self.parts[0]
        rows, width = first.keep[0].shape[1:]
        if self.lazy:
            shapes = [give.shape for give in self.gives]
            return [(give, None, i) for i, give in enumerate(self.gives)], shapes
        if self.merge or not first.route:
            if self.single and not self.merge:
                a, b = self.parts
                return [(a, [0], 0), (b, [0], 1)], [(1, rows, width)] * 2
            parts = self.parts[:1] if self.single else self.parts
            jobs = [(part, [0], 0) for part in parts]
            return jobs, [(len(parts), rows, width)]
        jobs, outs = [], []
        for part in self.parts:
            axis, step = part.route[0]
            which = 0 if axis == "shard" else 1
            stay = [i for i, label in enumerate(part.labels) if not label[which] & step]
            leave = [i for i, label in enumerate(part.labels) if label[which] & step]
            for blocks in (stay, leave):
                jobs.append((part, blocks, len(outs)))
                outs.append((len(blocks), rows, width))
        return jobs, outs

    def take(self, outs):
        if self.every is not None:
            return []
        net = self.net
        if self.lazy:
            self.lazy = False
            self.gots = [net.swap(give, "shard", 1) for give in outs]
            self.arm()
            return list(outs)
        if self.merge or not self.parts[0].route:
            if self.single and not self.merge:
                self.merge = True
                axis, step = self.last
                self.parts[0].keep = (outs[0], 0)
                self.parts[0].got = (net.swap(outs[1], axis, step), 0)
                return [outs[1]]
            mine = outs[0]
            self.every = [mine]
            self.every += [net.swap(mine, "replica", step) for step in range(1, net.replicas)]
            return [mine]
        sent = []
        for part, (keep, give) in zip(self.parts, zip(outs[::2], outs[1::2])):
            (axis, step), part.route = part.route[0], part.route[1:]
            which = 0 if axis == "shard" else 1
            part.labels = [label for label in part.labels if not label[which] & step]
            part.keep = (keep, 0)
            part.got = (net.swap(give, axis, step), 0)
            sent.append(give)
        return sent


class Line:
    def __init__(self, net, value, axes, sums=False, lower_at=None):
        self.net = net
        self.value = value
        self.sums = sums
        self.lower_at = lower_at
        self.route = [(axis, step) for axis in axes for step in net.bits(axis)[::-1]]
        self.count = 0
        self.full = None
        self.got = None
        self.over = False
        self.sent = self.send()

    def send(self):
        if not self.route:
            self.over = True
            return []
        axis, step = self.route.pop(0)
        self.got = self.net.swap(self.value, axis, step)
        return [self.value]

    def outs(self):
        if self.over:
            return []
        dims = self.value.shape
        if not self.sums:
            dims = (2 * dims[0],) + dims[1:]
        outs = [shape_of(dims, self.value.dtype)]
        if self.count + 1 == self.lower_at:
            outs.append(shape_of(dims, low_type))
        return outs

    def take(self, outs):
        if self.over:
            return []
        self.count += 1
        self.value = outs[0]
        if self.count == self.lower_at:
            self.full, self.value = outs
        return self.send()

    def end(self):
        while not self.over:
            if self.sums:
                both = self.value + self.got
            else:
                both = jnp.concatenate([self.value, self.got])
            self.take([both.astype(out.dtype) for out in self.outs()])
        return self.value


def line_kernel(sums, value_ref, got_ref, *out_refs):
    count = value_ref.shape[0]
    for out_ref in out_refs:
        if sums:
            out_ref[...] = value_ref[...] + got_ref[...]
        else:
            out_ref[:count] = value_ref[...].astype(out_ref.dtype)
            out_ref[count:] = got_ref[...].astype(out_ref.dtype)


def round_kernel(jobs, line_jobs, *refs):
    for sums, value, got, outs in line_jobs:
        line_kernel(sums, refs[value], refs[got], *[refs[out] for out in outs])
    place = [0] * 64
    for keep, got, blocks, keep_at, got_at, out in jobs:
        if blocks is None:
            refs[out][...] = refs[keep][...]
            continue
        for block in blocks:
            refs[out][place[out]] = (
                refs[keep][keep_at + block].astype(wide) + refs[got][got_at + block].astype(wide)
            ).astype(low_type)
            place[out] += 1


def run_round(folds, lines=(), after=()):
    arrays, jobs, shapes, counts = [], [], [], []

    def slot(array):
        for i, known in enumerate(arrays):
            if known is array:
                return i
        arrays.append(array)
        return len(arrays) - 1

    listed = []
    for fold in folds:
        fold_jobs, outs = fold.jobs()
        for part, blocks, out in fold_jobs:
            if blocks is None:
                place = slot(part)
                listed.append((place, place, None, 0, 0, len(shapes) + out))
                continue
            keep, keep_at = part.keep
            got, got_at = part.got
            listed.append((slot(keep), slot(got), blocks, keep_at, got_at, len(shapes) + out))
        shapes += outs
        counts.append(len(outs))
    shapes = [shape_of(dims, low_type) for dims in shapes]
    line_listed = []
    for line in lines:
        outs = line.outs()
        if outs:
            places = range(len(shapes), len(shapes) + len(outs))
            line_listed.append((line.sums, slot(line.value), slot(line.got), places))
            shapes += outs
        counts.append(len(outs))
    if not shapes:
        return []
    first_out = len(arrays) + len(after)
    jobs = [job[:5] + (first_out + job[5],) for job in listed]
    line_jobs = [job[:3] + ([first_out + i for i in job[3]],) for job in line_listed]
    outs = pl.pallas_call(
        functools.partial(round_kernel, jobs, line_jobs),
        in_specs=[pl.BlockSpec(memory_space=pltpu.VMEM)] * len(arrays)
        + [pl.BlockSpec(memory_space=pl.ANY)] * len(after),
        out_specs=[pl.BlockSpec(memory_space=pltpu.VMEM)] * len(shapes),
        out_shape=shapes,
        compiler_params=pltpu.CompilerParams(vmem_limit_bytes=58 * 2**20),
        name="round",
    )(*arrays, *after)
    sent = []
    for fold, count in zip(list(folds) + list(lines), counts):
        sent += fold.take(outs[:count])
        outs = outs[count:]
    return sent


def finish_kernel(steps, here_ref, *refs):
    ins, (qkv_ref, proj_ref, up_ref, down_ref, back_ref, at_ref, ff_ref) = refs[:-7], refs[-7:]
    rows, width = proj_ref.shape[1:]
    ins, parts = ins[: 2 * SLABS * LAYERS], ins[2 * SLABS * LAYERS :]
    for step, part in zip(steps, parts):
        back_ref[jnp.bitwise_xor(here_ref[0], step)] = part[...]
    for layer in range(LAYERS):
        at, ff = ins[:SLABS], ins[SLABS : 2 * SLABS]
        ins = ins[2 * SLABS :]
        for step in range(SLABS):
            place = jnp.bitwise_xor(here_ref[1], step)
            at_ref[place] = at[step][0]
            ff_ref[place] = ff[step][...]
        for place in range(SLABS):
            cols = slice(place * width, (place + 1) * width)
            if place < 3:
                qkv_ref[layer, :, cols] = at_ref[place].astype(wide)
            else:
                proj_ref[layer] = at_ref[place].astype(wide)
            up_ref[layer, :, cols] = ff_ref[place, 0].astype(wide)
            down_ref[layer, place * rows : (place + 1) * rows] = ff_ref[place, 1].astype(wide)


def finish(here, owned, back, steps):
    arrays = [part for at, ff in owned for part in (*at, *ff)] + back
    rows, width = owned[0][0][0].shape[1:]
    outs = [
        shape_of((LAYERS, rows, 3 * width), wide),
        shape_of((LAYERS, rows, width), wide),
        shape_of((LAYERS, rows, SLABS * width), wide),
        shape_of((LAYERS, SLABS * rows, width), wide),
        shape_of((len(back),) + back[0].shape, wide),
    ]
    return pl.pallas_call(
        functools.partial(finish_kernel, steps),
        grid_spec=pltpu.PrefetchScalarGridSpec(
            num_scalar_prefetch=1,
            grid=(1,),
            in_specs=[full(part.shape) for part in arrays],
            out_specs=[full(out.shape) for out in outs],
            scratch_shapes=[
                pltpu.VMEM((SLABS, rows, width), low_type),
                pltpu.VMEM((SLABS, 2, rows, width), low_type),
            ],
        ),
        out_shape=outs,
        compiler_params=pltpu.CompilerParams(vmem_limit_bytes=58 * 2**20),
        name="finish",
    )(here, *arrays)


def finish_plain(here, owned, places):
    found = [[], [], [], []]
    order = jnp.bitwise_xor(jnp.arange(places, dtype=jnp.int32), here[1])
    for at, ff in owned:
        at = jnp.take(jnp.stack(at), order, axis=0)[:, 0].astype(wide)
        ff = jnp.take(jnp.stack(ff), order, axis=0).transpose(1, 0, 2, 3).astype(wide)
        width = at.shape[-1]
        at = at.reshape(SLABS, -1, width)
        ff = ff.reshape(2, SLABS, -1, width)
        rows = at.shape[1]
        found[0].append(at[:3].transpose(1, 0, 2).reshape(rows, 3 * width))
        found[1].append(at[3])
        found[2].append(ff[0].transpose(1, 0, 2).reshape(rows, SLABS * width))
        found[3].append(ff[1].reshape(SLABS * rows, width))
    return [jnp.stack(each) for each in found]


def place_kernel(here_ref, own_ref, own_far_ref, *refs):
    near, far, out_ref = refs[:4], refs[4:8], refs[8]
    replica = here_ref[1]
    pair = pl.program_id(0) // 2
    odd = pl.program_id(0) % 2
    half = out_ref.shape[3] // 2
    for parity, own, parts in ((0, own_ref, near), (1, own_far_ref, far)):

        @pl.when(jnp.logical_and(pair == 0, odd == parity))
        def _():
            for place in range(SLABS):
                out_ref[place, 0] = own[place]

        @pl.when(jnp.logical_and(pair > 0, odd == parity))
        def _():
            for part, steps, low in zip(parts, ((0, 1), (2, 3), (0, 2), (1, 3)), (0, 0, half, half)):
                for i, step in enumerate(steps):
                    place = jnp.bitwise_xor(replica, step)
                    for k in range(out_ref.shape[2]):
                        out_ref[place, 0, k, low : low + half] = part[i, 0, k]


def place_weights(net, here, own, own_far, near, far):
    places, kinds, rows, width = own.shape
    half = rows // 2
    whole = pl.BlockSpec(own.shape, lambda g, here_ref: (0, 0, 0, 0))
    part = pl.BlockSpec(
        (2, 1, kinds, half, width),
        lambda g, here_ref: (0, jnp.maximum(g // 2 - 1, 0), 0, 0, 0),
    )

    def target(g, here_ref):
        pair = g // 2
        step = (pair % 2) * 4 + (pair // 2) * 2 + g % 2
        return (0, jnp.bitwise_xor(here_ref[0], step), 0, 0, 0)

    return pl.pallas_call(
        place_kernel,
        grid_spec=pltpu.PrefetchScalarGridSpec(
            num_scalar_prefetch=1,
            grid=(net.shards,),
            in_specs=[whole, whole] + [part] * 8,
            out_specs=pl.BlockSpec((places, 1, kinds, rows, width), target),
        ),
        out_shape=shape_of((places, net.shards, kinds, rows, width), low_type),
        compiler_params=pltpu.CompilerParams(vmem_limit_bytes=56 * 2**20),
        name="place_weights",
    )(here, own, own_far, *near, *far)


def gather_steps(net, here, packed):
    own_far = net.swap(packed, "shard", 1)
    mine = lax.dynamic_index_in_dim(packed, here[1], 0, keepdims=True)
    got = net.swap(mine, "shard", 4)
    yield [mine]
    both = jnp.concatenate([mine, got])
    more = net.swap(both, "shard", 2)
    yield [both]
    half = packed.shape[2] // 2
    halves = []
    for cut in (slice(0, half), slice(half, None)):
        halves.append(jnp.concatenate([got[:, :, cut], more[:, :, cut]])[None])
    gots = [net.swap(part, "replica", step) for part, step in zip(halves, (1, 2))]
    yield halves
    firsts = [jnp.concatenate([part, came]) for part, came in zip(halves, gots)]
    seconds = [net.swap(part, "replica", step) for part, step in zip(firsts, (2, 1))]
    firsts_far = [net.swap(part, "shard", 1) for part in firsts]
    yield firsts
    seconds_far = [net.swap(part, "shard", 1) for part in seconds]
    yield seconds
    near = [firsts[0], seconds[0], firsts[1], seconds[1]]
    far = [firsts_far[0], seconds_far[0], firsts_far[1], seconds_far[1]]
    return place_weights(net, here, packed, own_far, near, far)


def gather_whole(net, here, packed):
    mine = lax.dynamic_index_in_dim(packed, here[1], 0, keepdims=False)
    flat = mine.reshape(-1, mine.shape[-1])
    whole = lax.all_gather(flat, ("replica", "shard"), axis=0, tiled=True)
    return whole.reshape((net.replicas, net.shards) + mine.shape)


def plain_slabs(net, whole, tall_kind):
    places, shards, kinds, part, width = whole.shape
    split = whole.reshape(SLABS, places // SLABS, shards, kinds, part, width)
    split = split.transpose(3, 0, 2, 1, 4, 5).reshape(kinds, SLABS, shards, -1, width)
    made = []
    for kind in range(kinds):
        each = split[kind]
        if kind == tall_kind:
            each = each.transpose(1, 0, 2, 3)
        made.append(each.reshape(SLABS, 1, width, width))
    return jnp.stack(made, axis=2)


class Steps:
    def __init__(self, steps):
        self.steps = steps
        self.result = None
        self.over = False

    def go(self, count=1):
        sent = []
        for _ in range(count):
            if not self.over:
                try:
                    sent = next(self.steps)
                except StopIteration as end:
                    self.over = True
                    self.result = end.value
                    sent = []
        return list(sent)

    def end(self):
        while not self.over:
            self.go()
        return self.result


def local(
    net,
    hidden_in,
    condition,
    latent_live,
    out_grad,
    ada_weight,
    qkv_weight,
    proj_weight,
    fc1_weight,
    fc2_weight,
    ada_bias,
    qv_bias,
    proj_bias,
    fc1_bias,
    fc2_bias,
):
    shard = lax.axis_index("shard")
    replica = lax.axis_index("replica")
    here = jnp.stack([shard, replica]).astype(jnp.int32)
    shards, replicas = net.shards, net.replicas
    latents_here, model_width = condition.shape
    rows = proj_weight.shape[1]
    piece_rows = rows * SLABS // replicas
    mod_width = ada_weight.shape[2]

    fused = replicas == SLABS and shards == 2 * SLABS and rows % 16 == 0

    def pack(layer):
        qkv = qkv_weight[layer].astype(low_type)
        up = fc1_weight[layer].astype(low_type)
        down = fc2_weight[layer].astype(low_type)
        columns = lambda w, b: w[:, b * model_width : (b + 1) * model_width]
        attn = [columns(qkv, b) for b in range(3)] + [proj_weight[layer].astype(low_type)]
        kinds = [jnp.stack(attn), jnp.stack([columns(up, b) for b in range(SLABS)]), down]
        return [kind.reshape(replicas, 1, piece_rows, model_width) for kind in kinds]

    packs = [pack(layer) for layer in range(LAYERS)]
    if fused:
        a0, a1 = [Steps(gather_steps(net, here, kinds[0])) for kinds in packs]
        later = gather_whole(net, here, jnp.concatenate(packs[0][1:] + packs[1][1:], axis=1))
    else:
        wholes = [
            plain_slabs(net, gather_whole(net, here, jnp.concatenate(kinds, axis=1)), 2)
            for kinds in packs
        ]

    cond_low = jax.nn.silu(condition).astype(low_type)
    bias_rows = jnp.concatenate([qv_bias, proj_bias, fc1_bias, fc2_bias], axis=1).astype(low_type)
    bias_width = bias_rows.shape[1]
    bias_rows = jnp.pad(bias_rows, ((0, 0), (0, model_width - bias_width)))
    both_rel = net.gather_rel(jnp.concatenate([cond_low, bias_rows]), ["shard"])
    cond_rel = both_rel[:, :latents_here]
    found = net.order("shard")
    spots = jnp.array([found.index(step) for step in range(shards)], jnp.int32)
    order = jnp.take(spots, jnp.bitwise_xor(jnp.arange(shards, dtype=jnp.int32), here[0]))
    bias_all = jnp.take(both_rel[:, latents_here:], order, axis=0)
    group = shards * latents_here
    cond_line = Line(net, cond_rel.reshape(1, group, model_width), ["replica"])
    cond_rows = lax.dynamic_slice_in_dim(
        cond_rel.reshape(group, model_width), shard * rows, rows, axis=1
    )
    ada_low = ada_weight.astype(low_type)
    partial = jnp.stack([nn(cond_rows, ada_low[layer]) for layer in range(LAYERS)], axis=1)
    ada_part = ada_bias.shape[1]
    bias_here = lax.dynamic_update_slice_in_dim(
        jnp.zeros((LAYERS, mod_width), wide),
        ada_bias.astype(low_type).astype(wide),
        shard * ada_part,
        axis=1,
    )
    partial = (partial + bias_here[None]).reshape(shards, latents_here, LAYERS, mod_width)
    modulations = net.scatter_rel(partial)

    widths = (qv_bias.shape[1], proj_bias.shape[1], fc1_bias.shape[1], fc2_bias.shape[1])
    starts = (0, widths[0], widths[0] + widths[1], widths[0] + widths[1] + widths[2])

    def biases_of(layer):
        qv, proj, up, down = [
            bias_all[:, layer, start : start + width].reshape(-1).astype(wide)
            for start, width in zip(starts, widths)
        ]
        qkv_b = jnp.stack([qv[:model_width], jnp.zeros((model_width,), wide), qv[model_width:]])
        up_b = up.reshape(SLABS, 1, model_width)
        return (qkv_b[:, None], proj[None], up_b, down[None])

    def attn_first():
        return (a0.end(), 0), []

    if fused:
        attn_calls = (attn_first, lambda: ((a1.end(), 0), []))
        feed_calls = (
            lambda: ((later, 0), (later, 1), [a1.end()]),
            lambda: ((later, 2), (later, 3), []),
        )
        slot_calls = [lambda: []] * LAYERS
    else:
        attn_calls = [lambda w=w: ((w, 0), []) for w in wholes]
        feed_calls = [lambda w=w: ((w, 1), (w, 2), []) for w in wholes]
        slot_calls = [lambda: []] * LAYERS

    live_rows = latent_live.astype(wide)[:, None, None]
    saved_all = []
    current = hidden_in
    weights_all = []
    for layer in range(LAYERS):
        current, saved_state, layer_weights = forward_layer(
            here,
            current,
            modulations[:, layer].reshape(latents_here, 6, model_width),
            attn_calls[layer],
            feed_calls[layer],
            biases_of(layer),
            slot_calls[layer],
        )
        saved_all.append(saved_state)
        weights_all.append(layer_weights)
    result = current * live_rows
    grad_now = out_grad * live_rows

    def send(grads, lazy):
        if fused:
            return Fold(net, list(zip(grads[::2], grads[1::2])), lazy)
        slabs = [grads[0].reshape(SLABS, shards, rows, model_width)]
        if len(grads) > 1:
            down = grads[1].reshape(shards, SLABS, rows, model_width)
            slabs.append(down.transpose(1, 0, 2, 3))
        pairs = [[half[0] for half in order_grads(net, here, each)] for each in slabs]
        return Steps(reduce_steps(net, here, pairs))

    sends = {}
    bias_line = [None]

    def bias_row(layer, sums, up_sums, down_sums):
        grads = (
            jnp.concatenate([sums[0], sums[2]]),
            sums[3],
            up_sums.reshape(-1),
            down_sums[0],
        )
        bias_sums[layer] = jnp.concatenate([grad.reshape(shards, -1) for grad in grads], axis=1)
        if layer == 0:
            bias_line[0] = Line(net, jnp.stack(bias_sums), ["shard", "replica"], sums=True)

    def middle_slot(layer):
        def slot(ff_grads):
            fold = sends["ff", layer] = send(ff_grads, layer == 0)
            if not fused:
                return []
            if layer == 1:
                return fold.sent
            return run_round([sends["ff", 1], sends["at", 1], fold])

        return slot

    def late_slot(layer):
        def slot(sums, up_sums, down_sums):
            bias_row(layer, sums, up_sums, down_sums)
            if not fused:
                return []
            if layer == 1:
                return run_round([sends["ff", 1]], [cond_line])
            return bias_line[0].sent + run_round([sends["ff", 1], sends["at", 1], sends["ff", 0]])

        return slot

    ada_wide = ada_low.astype(wide)
    grad_cond = jnp.zeros((group, rows), wide)
    ada_grads = [None] * LAYERS
    modul_grads = [None] * LAYERS
    bias_sums = [None] * LAYERS
    for layer in reversed(range(LAYERS)):
        before = []
        if layer == 0 and fused:
            before = run_round([sends["ff", 1], sends["at", 1]], [cond_line])
        grad_now, grad_modul, at_grads = backward_layer(
            here,
            fused,
            grad_now,
            weights_all[layer],
            saved_all[layer],
            before,
            middle_slot(layer),
            late_slot(layer),
        )
        sends["at", layer] = send(at_grads, layer == 1)
        modul_grads[layer] = grad_modul
    lines = [
        bias_line[0],
        cond_line,
        Line(
            net,
            jnp.concatenate(modul_grads)[None],
            ["shard", "replica"],
            lower_at=len(net.bits("shard")),
        ),
    ]
    if fused:
        ring = [sends["ff", 1], sends["at", 1], sends["ff", 0], sends["at", 0]]
        while any(fold.every is None for fold in ring) or not all(line.over for line in lines):
            run_round(ring, lines)
    bias_total, cond_all, modul_low = [line.end() for line in lines]
    modul = lines[2].full
    modul_low = modul_low.reshape((replicas, shards) + modul_low.shape[1:])
    cond_every = lax.dynamic_slice_in_dim(
        cond_all.reshape(replicas * group, model_width), shard * rows, rows, axis=1
    )
    per_layer = lambda w, layer: w[..., layer * latents_here : (layer + 1) * latents_here, :]
    for layer in range(LAYERS):
        mine = per_layer(modul, layer).reshape(group, mod_width)
        grad_cond = grad_cond + exact_trail(mine, ada_wide[layer])
        every = per_layer(modul_low, layer).reshape(replicas * group, mod_width)
        ada_grads[layer] = tn(cond_every, every)
    own_mod = lax.dynamic_slice_in_dim(modul_low, shard * ada_part, ada_part, axis=3).astype(wide)
    own_mod = own_mod.reshape(replicas * shards, LAYERS, latents_here, ada_part)
    ada_bias_out = jnp.sum(own_mod, axis=(0, 2))
    bias_mine = lax.dynamic_index_in_dim(bias_total, shard, 1, keepdims=False)
    bias_out = [bias_mine[:, start : start + width] for start, width in zip(starts, widths)]

    parts = grad_cond.reshape(shards, latents_here, rows)
    back = [parts[0]]
    back += [net.swap(parts[i], "shard", found[i]) for i in range(1, shards)]
    if fused:
        owned = [(sends["at", layer].every, sends["ff", layer].every) for layer in range(LAYERS)]
        *weight_outs, back = finish(here, owned, back, found)
    else:
        owned = [
            (sends["at", layer].end(), sends["ff", layer].end()) for layer in range(LAYERS)
        ]
        weight_outs = finish_plain(here, owned, replicas)
        back = jnp.take(jnp.stack(back), order, axis=0)
    cond_back = back.transpose(1, 0, 2).reshape(latents_here, model_width)
    grad_condition = jax.vjp(jax.nn.silu, condition)[1](cond_back)[0]
    return (
        result,
        grad_now,
        grad_condition,
        jnp.stack(ada_grads),
        *weight_outs,
        ada_bias_out,
        *bias_out,
    )


def solution(mesh):
    tokens = P(("replica", "shard"), None, None)
    weight = P(None, "shard", None)
    bias = P(None, "shard")
    rows = P(("replica", "shard"), None)
    return jax.shard_map(
        functools.partial(local, Net(mesh)),
        mesh=mesh,
        in_specs=(tokens, rows, P(("replica", "shard")), tokens) + (weight,) * 5 + (bias,) * 5,
        out_specs=(tokens, tokens, rows) + (weight,) * 5 + (bias,) * 5,
        check_vma=False,
    )
```
